512 devices in a mesh: seq: 32 (over z, core), head: 16 (over y, x).
Axes of the slice: x: 4, y: 4, z: 16, core: 2. Of those that a mesh axis runs over, the one named last changes fastest.
Arguments:
- queries: bfloat16 [65536, 2048], P('seq', 'head'), may hold values from -64 to 64
- keys: bfloat16 [65536, 2048], P('seq', 'head'), may hold values from -24 to 24
- values: bfloat16 [65536, 2048], P('seq', 'head'), may hold values from -6 to 6
- d_out: bfloat16 [65536, 2048], P('seq', 'head'), may hold values from -6 to 6
- cluster_id: int32 [65536, 1], P('seq'), may hold values from 0 to 255; in each aligned block of 2048 rows (0 to 2047, 2048 to 4095, ...) at most 12 rows name the same one
Outputs:
- attn_out: bfloat16 [65536, 2048], P('seq', 'head')
- d_queries: bfloat16 [65536, 2048], P('seq', 'head')
- d_keys: bfloat16 [65536, 2048], P('seq', 'head')
- d_values: bfloat16 [65536, 2048], P('seq', 'head')
- centroids: float32 [256, 2048], P(None, 'head')
The draws below stay inside these ranges and needn't reach their ends.
Inputs may be any that keep to these rules, and one draw needn't show every extreme that they name: `cluster_id`: among the 2048 tokens of one device no cluster appears more than 12 times, and in every draw some cluster appears exactly 12 times among the tokens of some device; every cluster has at least one token.
All inputs are finite; a program needn't handle non-finite values.
Results may differ from the reference program's by a relative error of at most 0.0051.
Values may be sent and summed in bfloat16 or wider, within the bound.
No kernel may reach another device: no remote copies, remote signals or barrier semaphores. Data moves between devices by JAX's collectives and lax.ppermute only.
A program may use at most 64 MiB of HBM per device.

```python
import math
import jax
import jax.numpy as jnp
import numpy as np
from jax import lax

H = 16
DH = 128
CLUSTERS = 256
TOK_DEV = 2048
CAPC = 12
D = 2048
TOKENS = 65536
SLOTS = 384
N_SEQ = 32


def key_material(key):
    first, second, third = jax.random.split(key, 3)
    base_draw = jax.random.normal(first, (TOKENS, H * DH), jnp.float32)
    row_scale = jnp.exp(jax.random.uniform(second, (TOKENS, 1), jnp.float32, math.log(0.5), math.log(3.0)))
    column_scale = jnp.exp(jax.random.uniform(third, (1, H * DH), jnp.float32, math.log(0.5), math.log(2.0)))
    return base_draw * row_scale * column_scale


def draw_keys(key, part):
    material = key_material(key)
    return jnp.clip(material, -24.0, 24.0).astype(jnp.bfloat16)


def draw_queries(key, part):
    key = jax.random.fold_in(key, 3)
    first = jax.random.fold_in(key, 0)
    own_draw = jnp.clip(jax.random.normal(first, (TOKENS, H * DH), jnp.float32), -6.0, 6.0)
    return jnp.clip(own_draw, -64.0, 64.0).astype(jnp.bfloat16)


def level_of(key, dims, shards, least, top_value):
    def one(dim, shards_of):
        steps = jax.random.uniform(jax.random.fold_in(jax.random.fold_in(key, 6), dim), (shards_of,), jnp.float32, least / len(shards), top_value / len(shards))
        return jnp.repeat(jnp.exp(steps), dims[dim] // shards_of).reshape((-1,) + (1,) * (len(dims) - dim - 1))

    loudness = one(*shards[0])
    for cut in shards[1:]:
        loudness = loudness * one(*cut)
    return loudness


def shared_out(rng, own, number, rows, number_of, top, limit, lean):
    order = jax.random.permutation(rng, number_of)
    packed, ordinary = load_shares(number_of, rows * top, limit, lean, True), load_shares(number_of, rows * top, limit, lean, False)
    places = jnp.arange(number_of)

    def named(tallies, offset_by):
        used = int((tallies > 0).sum())
        fixed = max(1, used // 4)
        moved = fixed + (places - fixed + offset_by * (used - fixed)) % max(1, number_of - fixed)
        return jnp.zeros((number_of,), jnp.int32).at[order[jnp.where(places < fixed, places, moved)]].set(jnp.asarray(tallies, jnp.int32))

    tallies = jnp.where(number % 4 == 0, named(packed, number // 4), named(ordinary, number - number // 4 - 1))
    mixed = jax.random.permutation(jax.random.fold_in(own, 3), number_of)
    giver, receiver = mixed[0:number_of // 2 * 2:2], mixed[1:number_of // 2 * 2:2]
    margin = jnp.minimum(tallies[giver] - 1, limit - tallies[receiver]) // 2
    margin = jnp.where((giver == order[0]) | (receiver == order[0]) | (tallies[receiver] == 0), 0, jnp.maximum(margin, 0))
    moved = jax.random.randint(jax.random.fold_in(own, 4), (number_of // 2,), 0, 1 << 20) % (margin + 1)
    tallies = tallies.at[giver].add(-moved).at[receiver].add(moved)
    members = jnp.searchsorted(jnp.cumsum(tallies), jnp.arange(rows * top), side="right").astype(jnp.int32)
    listing = members.reshape(top, rows).T
    listing = listing[jax.random.permutation(jax.random.fold_in(own, 1), rows)]
    offset_by = jax.random.randint(jax.random.fold_in(own, 2), (rows, 1), 0, top)
    return jnp.take_along_axis(listing, (jnp.arange(top)[None, :] + offset_by) % top, axis=1)


def load_shares(amount, total, limit, skew, full):
    portions = [(1 << 20) // math.isqrt(grade ** skew) + 1 for grade in range(1, amount + 1)]
    largest = limit if full else min(limit, max(-(-total // amount), total * portions[0] // sum(portions)))
    least = 1 if total - largest >= amount - 1 else 0
    given, spare = [largest] + [least] * (amount - 1), total - largest - least * (amount - 1)
    while spare > 0:
        movable = [i for i in range(1, amount) if given[i] < largest] or [i for i in range(1, amount) if given[i] < limit]
        pool, remaining = sum([portions[i] for i in movable]), spare
        for i in movable:
            addition = min(limit - given[i], max(1, remaining * portions[i] // pool), spare)
            given[i] = given[i] + addition
            spare = spare - addition
    return np.array(given)


def centred(key, dims, spread, reach, cuts=(), kind=jnp.bfloat16):
    result = jax.random.normal(key, dims, jnp.float32) * spread
    if len(cuts) > 0:
        result = level_of(key, dims, cuts, -0.22, 0.18) * result
    return jnp.clip(result, min=-reach, max=reach).astype(kind)


def setup_inputs(seed: int = 0) -> dict:
    seeds = jax.random.split(jax.random.key(seed), 6)
    queries = draw_queries(jax.random.fold_in(seeds[5], 71), 0)
    keys = draw_keys(jax.random.fold_in(seeds[5], 71), 0)
    values = centred(seeds[2], (TOKENS, D), 1.0, 6.0, ((0, 32), (1, 16)))
    d_out = centred(seeds[3], (TOKENS, D), 1.0, 6.0, ((0, 32), (1, 16)))
    cluster_id_keys = jax.random.split(jax.random.fold_in(seeds[4], 1), TOKENS // TOK_DEV)
    cluster_id_turns = jax.random.permutation(jax.random.fold_in(seeds[4], 3), TOKENS // TOK_DEV)
    cluster_id = jax.vmap(lambda own, number: shared_out(jax.random.fold_in(seeds[4], 2), own, number, TOK_DEV, CLUSTERS, 1, CAPC, 2))(cluster_id_keys, cluster_id_turns).reshape((TOKENS, 1))
    return dict(queries=queries, keys=keys, values=values, d_out=d_out, cluster_id=cluster_id)


EPSILON = 1e-06
NEGATIVE = -1e+30

def cluster_attention(query_rows, key_rows, value_rows, grad_rows, visible):
    query_heads = query_rows.astype(jnp.float32).reshape(SLOTS, H, DH)
    key_heads = key_rows.astype(jnp.float32).reshape(SLOTS, H, DH)
    value_heads = value_rows.astype(jnp.float32).reshape(SLOTS, H, DH)
    grad_heads = grad_rows.astype(jnp.float32).reshape(SLOTS, H, DH)
    scaling = DH ** (-0.5)
    scores = jnp.einsum('shd,thd->hst', query_heads, key_heads) * scaling
    scores = jnp.where(visible[None], scores, NEGATIVE)
    row_top = lax.optimization_barrier(jnp.max(scores, axis=2, keepdims=True))
    weights = jnp.exp(scores - row_top)
    attention = weights / lax.optimization_barrier(jnp.sum(weights, axis=2, keepdims=True))
    attention_b = attention.astype(jnp.bfloat16).astype(jnp.float32)
    attended = jnp.einsum('hst,thd->shd', attention_b, value_heads).astype(jnp.bfloat16)
    grad_weights = jnp.einsum('shd,thd->hst', grad_heads, value_heads)
    row_delta = lax.optimization_barrier(jnp.sum(attention * grad_weights, axis=2, keepdims=True))
    grad_scores = (attention * (grad_weights - row_delta)).astype(jnp.bfloat16).astype(jnp.float32)
    grad_query = (jnp.einsum('hst,thd->shd', grad_scores, key_heads) * scaling).astype(jnp.bfloat16)
    grad_key = (jnp.einsum('hst,shd->thd', grad_scores, query_heads) * scaling).astype(jnp.bfloat16)
    grad_value = jnp.einsum('hst,shd->thd', attention_b, grad_heads).astype(jnp.bfloat16)
    return (attended.reshape(SLOTS, D), grad_query.reshape(SLOTS, D), grad_key.reshape(SLOTS, D), grad_value.reshape(SLOTS, D))

def reference(queries, keys, values, d_out, cluster_id):
    cluster_row = cluster_id[:, 0].astype(jnp.int32)
    member = (cluster_row.reshape(N_SEQ, TOK_DEV, 1) == jnp.arange(CLUSTERS, dtype=jnp.int32)[None, None, :]).astype(jnp.int32)
    ordinal = lax.optimization_barrier(jnp.sum((jnp.cumsum(member, axis=1) - 1) * member, axis=2)).reshape(TOKENS).astype(jnp.int32)
    device = (jnp.arange(TOKENS, dtype=jnp.int32) // TOK_DEV).astype(jnp.int32)
    slot_index = (cluster_row * SLOTS + device * CAPC + ordinal).astype(jnp.int32)
    token_of_slot = jnp.full((CLUSTERS * SLOTS,), TOKENS, jnp.int32).at[slot_index].set(jnp.arange(TOKENS, dtype=jnp.int32)).reshape(CLUSTERS, SLOTS)
    positions = jnp.arange(SLOTS, dtype=jnp.int32)
    row_index = positions[:, None]
    column_index = positions[None, :]

    def take_rows(source, slot_tokens):
        return jnp.take(source, slot_tokens, axis=0, mode='fill', fill_value=0)

    def scan_step(carry, slot_tokens):
        filled = slot_tokens < TOKENS
        visible = filled[None, :] & (column_index <= row_index) | (column_index == row_index)
        results = cluster_attention(take_rows(queries, slot_tokens), take_rows(keys, slot_tokens), take_rows(values, slot_tokens), take_rows(d_out, slot_tokens), visible)
        updated = tuple((held.at[slot_tokens].set(rows, mode='drop') for held, rows in zip(carry, results)))
        return (updated, None)
    start_values = tuple((jnp.zeros((TOKENS, D), jnp.bfloat16) for index in range(4)))
    (attn_out, d_queries, d_keys, d_values), unused = lax.scan(scan_step, start_values, token_of_slot)
    key_float = keys.astype(jnp.float32)
    unit_keys = key_float / jnp.sqrt(lax.optimization_barrier(jnp.mean(key_float * key_float, axis=1, keepdims=True)) + EPSILON)
    cluster_sums = jax.ops.segment_sum(unit_keys, cluster_row, num_segments=CLUSTERS)
    counts = jax.ops.segment_sum(jnp.ones((TOKENS,), jnp.float32), cluster_row, num_segments=CLUSTERS)
    cluster_means = cluster_sums / counts[:, None]
    centroids = cluster_means / jnp.sqrt(lax.optimization_barrier(jnp.mean(cluster_means * cluster_means, axis=1, keepdims=True)) + EPSILON)
    return (attn_out, d_queries, d_keys, d_values, centroids)
```

```python
import functools

import jax
import jax.numpy as jnp
from jax import lax
from jax.experimental import pallas as pl
from jax.experimental.pallas import tpu as pltpu
from jax.sharding import PartitionSpec as P

DH = 128
CLUSTERS = 256
CAPC = 12
D = 2048
N_SEQ = 32
OWN = CLUSTERS // N_SEQ
SLOTS = N_SEQ * CAPC
GROUP = 4
GROUPS = N_SEQ // GROUP
PIECE = GROUP * CAPC
ROWS_SHORT = 80
ROWS_FULL = OWN * CAPC
EPSILON = 1e-06
NEGATIVE = -1e30
VMEM = 56 * 1024 * 1024


def iota(shape, dim):
    return lax.broadcasted_iota(jnp.int32, shape, dim)


def one_hot(mask):
    return jnp.where(mask, 1.0, 0.0).astype(jnp.bfloat16)


def dot(a, b, ca, cb):
    return lax.dot_general(a, b, (((ca,), (cb,)), ((), ())), preferred_element_type=jnp.float32)


def pack_kernel(place_ref, q_ref, k_ref, v_ref, g_ref, out_ref, all_ref):
    step = pl.program_id(0)

    @pl.when(step == 0)
    def _():
        for i, ref in enumerate((q_ref, k_ref, v_ref, g_ref)):
            all_ref[:, i * DH : (i + 1) * DH] = ref[...]

    rows = out_ref.shape[0]
    wanted = iota((rows, place_ref.shape[1]), 0) + step * rows
    out_ref[...] = dot(one_hot(wanted == place_ref[...]), all_ref[...], 1, 0).astype(jnp.bfloat16)


def pack(place_row, arrays, rows):
    tokens = place_row.shape[1]
    whole = pl.BlockSpec((tokens, DH), lambda i: (0, 0))
    return pl.pallas_call(
        pack_kernel,
        grid=(GROUPS,),
        in_specs=[pl.BlockSpec((1, tokens), lambda i: (0, 0))] + [whole] * 4,
        out_specs=pl.BlockSpec((GROUP * rows, 4 * DH), lambda i: (i, 0)),
        out_shape=jax.ShapeDtypeStruct((N_SEQ * rows, 4 * DH), jnp.bfloat16),
        scratch_shapes=[pltpu.VMEM((tokens, 4 * DH), jnp.bfloat16)],
        compiler_params=pltpu.CompilerParams(vmem_limit_bytes=VMEM),
        name="pack",
    )(place_row, *arrays)


def unpack_kernel(place_ref, in_ref, *out_refs):
    tokens = place_ref.shape[0]
    chosen = one_hot(place_ref[...] == iota((tokens, in_ref.shape[0]), 1))
    rows = dot(chosen, in_ref[...], 1, 0).astype(jnp.bfloat16)
    for i, ref in enumerate(out_refs):
        ref[...] = rows[:, i * DH : (i + 1) * DH]


def unpack(place_column, block):
    tokens = place_column.shape[0]
    tile = 256
    return pl.pallas_call(
        unpack_kernel,
        grid=(tokens // tile,),
        in_specs=[
            pl.BlockSpec((tile, 1), lambda i: (i, 0)),
            pl.BlockSpec(block.shape, lambda i: (0, 0)),
        ],
        out_specs=[pl.BlockSpec((tile, DH), lambda i: (i, 0))] * 4,
        out_shape=[jax.ShapeDtypeStruct((tokens, DH), jnp.bfloat16)] * 4,
        compiler_params=pltpu.CompilerParams(vmem_limit_bytes=VMEM),
        name="unpack",
    )(place_column, block)


def attention_kernel(
    rows, place_ref, fill_ref, in_ref, out_ref, key_ref, square_ref, x_ref, y_ref, p_ref, s_ref
):
    part = GROUP * rows
    scaling = DH**-0.5

    def chosen(g):
        return one_hot(iota((part, OWN * PIECE), 0) == place_ref[pl.ds(g, 1), :])

    def spread(g, _):
        block = in_ref[pl.ds(pl.multiple_of(g * part, part), part), :]
        full = dot(chosen(g), block, 0, 0).astype(jnp.bfloat16)
        for k in range(OWN):
            at = pl.multiple_of(k * SLOTS + g * PIECE, 16)
            x_ref[pl.ds(at, PIECE), :] = full[k * PIECE : (k + 1) * PIECE]
        return 0

    lax.fori_loop(0, GROUPS, spread, 0)
    p_ref[...] = jnp.zeros_like(p_ref)
    s_ref[...] = jnp.zeros_like(s_ref)

    def attend(k, _):
        at = pl.ds(pl.multiple_of(k * SLOTS, SLOTS), SLOTS)
        query, key = x_ref[at, 0:DH], x_ref[at, DH : 2 * DH]
        value, grad = x_ref[at, 2 * DH : 3 * DH], x_ref[at, 3 * DH : 4 * DH]
        filled = fill_ref[pl.ds(k, 1), :]
        outs, grad_queries = [], []
        for i in range(SLOTS // DH):
            top, width = slice(i * DH, (i + 1) * DH), (i + 1) * DH
            scores = dot(query[top], key[:width], 1, 1) * scaling
            visible = (iota((DH, width), 1) <= iota((DH, width), 0) + i * DH) & (
                filled[:, :width] > 0.5
            )
            scores = jnp.where(visible, scores, NEGATIVE)
            weights = jnp.exp(scores - jnp.max(scores, axis=1, keepdims=True))
            attention = weights * (1.0 / jnp.sum(weights, axis=1, keepdims=True))
            rounded = attention.astype(jnp.bfloat16)
            p_ref[top, :width] = rounded
            outs.append(dot(rounded, value[:width], 1, 0))
            grad_weights = dot(grad[top], value[:width], 1, 1)
            delta = jnp.sum(attention * grad_weights, axis=1, keepdims=True)
            grad_scores = (attention * (grad_weights - delta)).astype(jnp.bfloat16)
            s_ref[top, :width] = grad_scores
            grad_queries.append(dot(grad_scores, key[:width], 1, 0) * scaling)
        y_ref[at, 0:DH] = jnp.concatenate(outs, axis=0).astype(jnp.bfloat16)
        y_ref[at, DH : 2 * DH] = jnp.concatenate(grad_queries, axis=0).astype(jnp.bfloat16)
        grad_key = dot(s_ref[...], query, 0, 0) * scaling
        y_ref[at, 2 * DH : 3 * DH] = grad_key.astype(jnp.bfloat16)
        y_ref[at, 3 * DH : 4 * DH] = dot(p_ref[...], grad, 0, 0).astype(jnp.bfloat16)
        key_ref[k] = key
        wide = key.astype(jnp.float32)
        square_ref[pl.ds(k, 1), :] = lax.dot_general(
            jnp.ones((8, DH), jnp.float32),
            wide * wide,
            (((1,), (1,)), ((), ())),
            precision=lax.Precision.HIGHEST,
            preferred_element_type=jnp.float32,
        )[0:1]
        return 0

    lax.fori_loop(0, OWN, attend, 0)

    def gather(g, _):
        pieces = [
            y_ref[pl.ds(pl.multiple_of(k * SLOTS + g * PIECE, 16), PIECE), :] for k in range(OWN)
        ]
        block = dot(chosen(g), jnp.concatenate(pieces, axis=0), 1, 0)
        out_ref[pl.ds(pl.multiple_of(g * part, part), part), :] = block.astype(jnp.bfloat16)
        return 0

    lax.fori_loop(0, GROUPS, gather, 0)


def attention(places, filled, block, rows):
    vmem = pl.BlockSpec(memory_space=pltpu.VMEM)
    return pl.pallas_call(
        functools.partial(attention_kernel, rows),
        in_specs=[vmem] * 3,
        out_specs=[vmem] * 3,
        out_shape=[
            jax.ShapeDtypeStruct(block.shape, jnp.bfloat16),
            jax.ShapeDtypeStruct((OWN, SLOTS, DH), jnp.bfloat16),
            jax.ShapeDtypeStruct((OWN, SLOTS), jnp.float32),
        ],
        scratch_shapes=[
            pltpu.VMEM((OWN * SLOTS, 4 * DH), jnp.bfloat16),
            pltpu.VMEM((OWN * SLOTS, 4 * DH), jnp.bfloat16),
            pltpu.VMEM((SLOTS, SLOTS), jnp.bfloat16),
            pltpu.VMEM((SLOTS, SLOTS), jnp.bfloat16),
        ],
        compiler_params=pltpu.CompilerParams(vmem_limit_bytes=VMEM),
        name="attention",
    )(places, filled, block)


def exchange(x, axis):
    return lax.all_to_all(x, axis, 0, 0, tiled=True)


def share(x, axis):
    return exchange(jnp.broadcast_to(x[None], (lax.axis_size(axis),) + x.shape), axis)


def body(queries, keys, values, d_out, cluster_id):
    seq = lax.axis_index("seq")
    member = (cluster_id == iota((1, CLUSTERS), 1)).astype(jnp.int32)
    running = jnp.cumsum(member, axis=0)
    ordinal = jnp.sum((running - 1) * member, axis=1, keepdims=True)
    own_counts = jnp.sum(member, axis=0)
    counts = share(own_counts[None].astype(jnp.float32), "seq")[:, 0].astype(jnp.int32)

    totals = jnp.sum(counts, axis=0)
    index = jnp.arange(CLUSTERS, dtype=jnp.int32)
    before = (totals[None, :] > totals[:, None]) | (
        (totals[None, :] == totals[:, None]) & (index[None, :] < index[:, None])
    )
    rank = jnp.sum(before.astype(jnp.int32), axis=1)
    turn = rank // N_SEQ
    owner = jnp.where(turn % 2 == 0, rank % N_SEQ, N_SEQ - 1 - rank % N_SEQ)
    same = owner[None, :] == owner[:, None]
    pair = jnp.sum(jnp.where(same[None], counts[:, None, :], 0), axis=2)
    earlier = same & (turn[None, :] < turn[:, None])
    start = jnp.sum(jnp.where(earlier[None], counts[:, None, :], 0), axis=2)
    mine = (owner[None, :] == seq) & (turn[None, :] == jnp.arange(OWN, dtype=jnp.int32)[:, None])
    here_counts = jnp.sum(jnp.where(mine[:, None, :], counts[None], 0), axis=2)
    here_start = jnp.sum(jnp.where(mine[:, None, :], start[None], 0), axis=2)
    start_me = lax.dynamic_index_in_dim(start, seq, 0, keepdims=False)

    def with_rows(rows, queries, keys, values, d_out):
        table = owner * rows + start_me
        place = ordinal + jnp.sum(member * table[None, :], axis=1, keepdims=True)
        sent = pack(place.reshape(1, -1), (queries, keys, values, d_out), rows)
        slot = jnp.arange(CAPC, dtype=jnp.int32)
        taken = slot[None, None, :] < here_counts[:, :, None]
        line = (jnp.arange(N_SEQ, dtype=jnp.int32) % GROUP) * rows
        spot = here_start[:, :, None] + slot[None, None, :] + line[None, :, None]
        spot = jnp.where(taken, spot, -1).reshape(OWN, GROUPS, PIECE)
        spot = spot.transpose(1, 0, 2).reshape(GROUPS, OWN * PIECE)
        filled = taken.reshape(OWN, SLOTS).astype(jnp.float32)
        received = exchange(sent.reshape(N_SEQ, rows, 4 * DH), "seq")
        results, key_rows, squares = attention(
            spot, filled, received.reshape(N_SEQ * rows, 4 * DH), rows
        )
        returned = exchange(results.reshape(N_SEQ, rows, 4 * DH), "seq")
        norm = jnp.sum(share(squares, "head"), axis=0)
        size = jnp.sum(here_counts, axis=1).astype(jnp.float32)
        unit = filled / jnp.sqrt(norm / D + EPSILON)
        means = jnp.sum(unit[:, :, None] * key_rows.astype(jnp.float32), axis=1) / size[:, None]
        spread = jnp.sum(share(jnp.sum(means * means, axis=1)[None], "head"), axis=0)[0]
        rows_here = means / jnp.sqrt(spread / D + EPSILON)[:, None]
        rows_all = share(rows_here, "seq").reshape(CLUSTERS, DH)
        centroids = rows_all[owner * OWN + turn]
        outs = unpack(place, returned.reshape(N_SEQ * rows, 4 * DH))
        return (*outs, centroids)

    return lax.cond(
        jnp.max(pair) <= ROWS_SHORT,
        functools.partial(with_rows, ROWS_SHORT),
        functools.partial(with_rows, ROWS_FULL),
        queries,
        keys,
        values,
        d_out,
    )


def solution(mesh):
    wide = P("seq", "head")
    return jax.shard_map(
        body,
        mesh=mesh,
        in_specs=(wide, wide, wide, wide, P("seq", None)),
        out_specs=(wide, wide, wide, wide, P(None, "head")),
        check_vma=False,
    )
```

```python
import functools

import jax
import jax.numpy as jnp
from jax import lax
from jax.experimental import pallas as pl
from jax.experimental.pallas import tpu as pltpu
from jax.sharding import PartitionSpec as P

DH = 128
CLUSTERS = 256
CAPC = 12
D = 2048
N_SEQ = 32
OWN = CLUSTERS // N_SEQ
SLOTS = N_SEQ * CAPC
GROUP = 4
GROUPS = N_SEQ // GROUP
PIECE = GROUP * CAPC
ROWS_SHORT = 72
ROWS_FULL = OWN * CAPC
EPSILON = 1e-06
HIDDEN = 1e30
LOG2E = 1.4426950408889634
TOGETHER = 4
VMEM = 24 * 1024 * 1024
VMEM_MOST = 60 * 1024 * 1024


def iota(shape, dim):
    return lax.broadcasted_iota(jnp.int32, shape, dim)


def one_hot(mask):
    return jnp.where(mask, 1.0, 0.0).astype(jnp.bfloat16)


def dot(a, b, ca, cb):
    return lax.dot_general(a, b, (((ca,), (cb,)), ((), ())), preferred_element_type=jnp.float32)


def pack_kernel(
    rows, seq_ref, plan_ref, cluster_ref, ordinal_ref, q_ref, k_ref, v_ref, g_ref,
    out_ref, place_ref, all_ref, part_ref, sem_ref,
):
    step = pl.program_id(0)
    part = GROUP * rows

    @pl.when(step == 0)
    def _():
        for i, ref in enumerate((q_ref, k_ref, v_ref, g_ref)):
            all_ref[:, i * DH : (i + 1) * DH] = ref[...]
        chosen = (iota((N_SEQ, CLUSTERS), 0) == seq_ref[0, 0])
        start = jnp.sum(jnp.where(chosen, plan_ref[:N_SEQ], 0.0), axis=0, keepdims=True)
        owner = plan_ref[N_SEQ : N_SEQ + 1]
        table = jnp.where(iota((8, CLUSTERS), 0) == 0, owner, start).astype(jnp.bfloat16)
        tokens = cluster_ref.shape[1]
        member = one_hot(iota((CLUSTERS, tokens), 0) == cluster_ref[...])
        found = dot(table, member, 1, 0)
        place = found[0:1] * rows + found[1:2]
        place_ref[...] = place.astype(jnp.int32) + ordinal_ref[...]

    def copy(slot, at):
        return pltpu.make_async_copy(
            part_ref.at[slot], out_ref.at[pl.ds(pl.multiple_of(at * part, part), part)], sem_ref.at[slot]
        )

    slot = lax.rem(step, 2)

    @pl.when(step >= 2)
    def _():
        copy(slot, step - 2).wait()

    wanted = iota((part, place_ref.shape[1]), 0) + step * part
    part_ref[slot] = dot(one_hot(wanted == place_ref[...]), all_ref[...], 1, 0).astype(jnp.bfloat16)
    copy(slot, step).start()

    @pl.when(step == GROUPS - 1)
    def _():
        copy(1 - slot, step - 1).wait()
        copy(slot, step).wait()


def pack(seq, planned, cluster_row, ordinal_row, arrays, rows):
    tokens = cluster_row.shape[1]

    def whole(*shape):
        return pl.BlockSpec(shape, lambda i: (0, 0))

    return pl.pallas_call(
        functools.partial(pack_kernel, rows),
        grid=(GROUPS,),
        in_specs=[
            pl.BlockSpec(memory_space=pltpu.SMEM),
            whole(*planned.shape),
            whole(1, tokens),
            whole(1, tokens),
        ]
        + [whole(tokens, DH)] * 4,
        out_specs=[pl.BlockSpec(memory_space=pltpu.HBM), whole(1, tokens)],
        out_shape=[
            jax.ShapeDtypeStruct((N_SEQ * rows, 4 * DH), jnp.bfloat16),
            jax.ShapeDtypeStruct((1, tokens), jnp.int32),
        ],
        scratch_shapes=[
            pltpu.VMEM((tokens, 4 * DH), jnp.bfloat16),
            pltpu.VMEM((2, GROUP * rows, 4 * DH), jnp.bfloat16),
            pltpu.SemaphoreType.DMA((2,)),
        ],
        compiler_params=pltpu.CompilerParams(vmem_limit_bytes=VMEM_MOST),
        name="pack",
    )(seq, planned, cluster_row, ordinal_row, *arrays)


def unpack_kernel(place_ref, in_ref, *out_refs):
    tokens = place_ref.shape[0]
    chosen = one_hot(place_ref[...] == iota((tokens, in_ref.shape[0]), 1))
    rows = dot(chosen, in_ref[...], 1, 0).astype(jnp.bfloat16)
    for i, ref in enumerate(out_refs):
        ref[...] = rows[:, i * DH : (i + 1) * DH]


def unpack(place_column, block):
    tokens = place_column.shape[0]
    tile = 256
    return pl.pallas_call(
        unpack_kernel,
        grid=(tokens // tile,),
        in_specs=[
            pl.BlockSpec((tile, 1), lambda i: (i, 0)),
            pl.BlockSpec(block.shape, lambda i: (0, 0)),
        ],
        out_specs=[pl.BlockSpec((tile, DH), lambda i: (i, 0))] * 4,
        out_shape=[jax.ShapeDtypeStruct((tokens, DH), jnp.bfloat16)] * 4,
        compiler_params=pltpu.CompilerParams(vmem_limit_bytes=VMEM),
        name="unpack",
    )(place_column, block)


def attention_kernel(rows, place_ref, in_ref, out_ref, x_ref, hide_ref, y_ref):
    part = GROUP * rows
    scaling = DH**-0.5

    def chosen(g):
        return one_hot(iota((part, OWN * PIECE), 0) == place_ref[pl.ds(g, 1), :])

    def spread(g, _):
        block = in_ref[pl.ds(pl.multiple_of(g * part, part), part), :]
        block = jnp.concatenate([block, jnp.ones((part, DH), jnp.bfloat16)], axis=1)
        full = dot(chosen(g), block, 0, 0)
        moved = full[:, : 4 * DH].astype(jnp.bfloat16)
        hide = (full[:, 4 * DH :] - 1.0) * HIDDEN
        for k in range(OWN):
            at = pl.ds(pl.multiple_of(k * SLOTS + g * PIECE, 16), PIECE)
            x_ref[at, :] = moved[k * PIECE : (k + 1) * PIECE]
            hide_ref[at, :] = hide[k * PIECE : (k + 1) * PIECE]
        return 0

    lax.fori_loop(0, GROUPS, spread, 0)
    causal = iota((DH, DH), 0) <= iota((DH, DH), 1)

    def attend(k):
        at = pl.ds(pl.multiple_of(k * SLOTS, SLOTS), SLOTS)
        query, key = x_ref[at, 0:DH], x_ref[at, DH : 2 * DH]
        value, grad = x_ref[at, 2 * DH : 3 * DH], x_ref[at, 3 * DH : 4 * DH]
        hide = hide_ref[at, :]
        weights_all, changes_all = [], []
        for i in range(SLOTS // DH):
            low, high = i * DH, (i + 1) * DH
            scores = dot(key[:high], query[low:high], 1, 1) * (scaling * LOG2E) + hide[:high]
            last = jnp.where(causal, scores[low:], -HIDDEN)
            scores = last if i == 0 else jnp.concatenate([scores[:low], last], axis=0)
            weights = jnp.exp2(scores - jnp.max(scores, axis=0, keepdims=True))
            attention = weights * (1.0 / jnp.sum(weights, axis=0, keepdims=True))
            grad_weights = dot(value[:high], grad[low:high], 1, 1)
            delta = jnp.sum(attention * grad_weights, axis=0, keepdims=True)
            weights_all.append(attention.astype(jnp.bfloat16))
            changes_all.append((attention * (grad_weights - delta)).astype(jnp.bfloat16))
        outs, grad_queries = [], []
        for i in range(SLOTS // DH):
            high = (i + 1) * DH
            outs.append(dot(weights_all[i], value[:high], 0, 0))
            grad_queries.append(dot(changes_all[i], key[:high], 0, 0) * scaling)
        grad_values, grad_keys = [], []
        for j in range(SLOTS // DH):
            row = slice(j * DH, (j + 1) * DH)
            rest = slice(j * DH, SLOTS)
            wide = jnp.concatenate([w[row] for w in weights_all[j:]], axis=1)
            grad_values.append(dot(wide, grad[rest], 1, 0))
            wide = jnp.concatenate([c[row] for c in changes_all[j:]], axis=1)
            grad_keys.append(dot(wide, query[rest], 1, 0) * scaling)
        for i, pieces in enumerate((outs, grad_queries, grad_keys, grad_values)):
            y_ref[at, i * DH : (i + 1) * DH] = jnp.concatenate(pieces, axis=0).astype(jnp.bfloat16)

    def attend_several(i, _):
        for j in range(TOGETHER):
            attend(i * TOGETHER + j)
        return 0

    lax.fori_loop(0, OWN // TOGETHER, attend_several, 0)

    def gather(g, _):
        pieces = [
            y_ref[pl.ds(pl.multiple_of(k * SLOTS + g * PIECE, 16), PIECE), :] for k in range(OWN)
        ]
        block = dot(chosen(g), jnp.concatenate(pieces, axis=0), 1, 0)
        out_ref[pl.ds(pl.multiple_of(g * part, part), part), :] = block.astype(jnp.bfloat16)
        return 0

    lax.fori_loop(0, GROUPS, gather, 0)


def attention(places, block, rows):
    vmem = pl.BlockSpec(memory_space=pltpu.VMEM)
    return pl.pallas_call(
        functools.partial(attention_kernel, rows),
        in_specs=[vmem] * 2,
        out_specs=vmem,
        out_shape=jax.ShapeDtypeStruct(block.shape, jnp.bfloat16),
        scratch_shapes=[
            pltpu.VMEM((OWN * SLOTS, 4 * DH), jnp.bfloat16),
            pltpu.VMEM((OWN * SLOTS, DH), jnp.float32),
            pltpu.VMEM((OWN * SLOTS, 4 * DH), jnp.bfloat16),
        ],
        compiler_params=pltpu.CompilerParams(vmem_limit_bytes=VMEM),
        name="attention",
    )(places, block)


def across(x, step):
    low = (iota(x.shape, 1) & step) == 0
    return jnp.where(low, pltpu.roll(x, x.shape[1] - step, 1), pltpu.roll(x, step, 1))


def plan_kernel(counts_ref, out_ref, most_ref):
    counts = counts_ref[...]
    size_row = jnp.sum(counts, axis=0, keepdims=True)
    size_column = dot(counts.astype(jnp.bfloat16), jnp.ones((N_SEQ, CLUSTERS), jnp.bfloat16), 0, 0)
    square = (CLUSTERS, CLUSTERS)
    before = (size_column > size_row) | (
        (size_column == size_row) & (iota(square, 0) < iota(square, 1))
    )
    rank = jnp.sum(jnp.where(before, 1.0, 0.0), axis=0, keepdims=True).astype(jnp.int32)
    turn, spot = lax.shift_right_logical(rank, 5), rank & (N_SEQ - 1)
    owner = jnp.where((turn & 1) == 0, spot, N_SEQ - 1 - spot)
    number = iota((8, CLUSTERS), 1).astype(jnp.float32)
    named = jnp.concatenate([counts, number], axis=0).astype(jnp.bfloat16)
    tables = []
    for k in range(OWN):
        here = jnp.where(turn == k, owner, -1)
        tables.append(dot(named, one_hot(iota((DH, CLUSTERS), 0) == here), 1, 1))
    load = functools.reduce(jnp.add, [t[:N_SEQ] for t in tables])

    def cost(x):
        over = jnp.maximum(x - 60.0, 0.0)
        over = over * over
        return over * over

    for step in (1, 2, 4, 8, 16):
        other = across(load, step)
        for k in range(OWN):
            theirs = across(tables[k], step)
            change = theirs[:N_SEQ] - tables[k][:N_SEQ]
            more, less = load + change, other - change
            gain = (cost(more) + cost(less)) - (cost(load) + cost(other))
            swap = jnp.sum(gain, axis=0, keepdims=True) < 0.0
            load = jnp.where(swap, more, load)
            other = jnp.where(swap, less, other)
            tables[k] = jnp.where(swap, theirs, tables[k])
    owners = iota((N_SEQ, DH), 1)
    load = jnp.where(owners < N_SEQ, load, 0.0)
    most_ref[...] = jnp.max(jnp.max(load, axis=1, keepdims=True), axis=0, keepdims=True)
    start = jnp.zeros((N_SEQ, DH), jnp.float32)
    result = jnp.zeros((N_SEQ + 8, CLUSTERS), jnp.float32)
    for k in range(OWN):
        names = tables[k][N_SEQ : N_SEQ + 1]
        names = jnp.where(owners[:1] < N_SEQ, names, -1.0).astype(jnp.int32)
        extra = jnp.where(iota((8, DH), 0) == 0, iota((8, DH), 1), k).astype(jnp.float32)
        values = jnp.concatenate([start, extra], axis=0).astype(jnp.bfloat16)
        result += dot(values, one_hot(iota((CLUSTERS, DH), 0) == names), 1, 1)
        start = start + tables[k][:N_SEQ]
    out_ref[...] = result


def plan(counts):
    return pl.pallas_call(
        plan_kernel,
        out_shape=[
            jax.ShapeDtypeStruct((N_SEQ + 8, CLUSTERS), jnp.float32),
            jax.ShapeDtypeStruct((1, 1), jnp.float32),
        ],
        compiler_params=pltpu.CompilerParams(vmem_limit_bytes=VMEM),
        name="plan",
    )(counts)


def exchange(x, axis):
    return lax.all_to_all(x, axis, 0, 0, tiled=True)


def share(x, axis):
    return exchange(jnp.broadcast_to(x[None], (lax.axis_size(axis),) + x.shape), axis)


def seq_gather(x, returned):
    swapped = lax.ppermute(x, "seq", [(i, i ^ 1) for i in range(N_SEQ)])
    x = jnp.stack([x, swapped])
    for stride in (1, 4):
        pieces = [x]
        for step in (1, 2, 3):
            away = 2 * stride * step
            pairs = [(i, (i + away) % N_SEQ) for i in range(N_SEQ)]
            pieces.append(lax.ppermute(x, "seq", pairs))
        x = jnp.concatenate(pieces, axis=0)
        if stride == 1:
            x, returned = lax.optimization_barrier((x, returned))
    return x, returned


def body(queries, keys, values, d_out, cluster_id):
    seq = lax.axis_index("seq")
    tokens = queries.shape[0]
    member = (cluster_id == iota((1, CLUSTERS), 1)).astype(jnp.int32)
    own_counts, cluster_id = lax.optimization_barrier((jnp.sum(member, axis=0), cluster_id))
    member = (cluster_id == iota((1, CLUSTERS), 1)).astype(jnp.int32)
    running = jnp.cumsum(member, axis=0)
    ordinal = jnp.sum((running - 1) * member, axis=1)
    counts = share(own_counts[None].astype(jnp.float32), "seq")[:, 0]
    counts, ordinal = lax.optimization_barrier((counts, ordinal))
    planned, most = plan(counts)

    def with_rows(rows, queries, keys, values, d_out):
        sent, place = pack(
            seq.reshape(1, 1),
            planned,
            cluster_id.reshape(1, tokens),
            ordinal.reshape(1, tokens),
            (queries, keys, values, d_out),
            rows,
        )
        received = exchange(sent.reshape(N_SEQ, rows, 4 * DH), "seq")
        plan_whole = planned.astype(jnp.int32)
        start, owner, turn = plan_whole[:N_SEQ], plan_whole[N_SEQ], plan_whole[N_SEQ + 1]
        turns = jnp.arange(OWN, dtype=jnp.int32)
        mine = (owner[None, :] == seq) & (turn[None, :] == turns[:, None])
        here_counts = jnp.sum(jnp.where(mine[:, None, :], counts[None], 0.0), axis=2)
        here_start = jnp.sum(jnp.where(mine[:, None, :], start[None], 0), axis=2)
        slot = jnp.arange(CAPC, dtype=jnp.int32)
        taken = slot[None, None, :] < here_counts.astype(jnp.int32)[:, :, None]
        line = (jnp.arange(N_SEQ, dtype=jnp.int32) % GROUP) * rows
        spot = here_start[:, :, None] + slot[None, None, :] + line[None, :, None]
        spot = jnp.where(taken, spot, -1).reshape(OWN, GROUPS, PIECE)
        spot = spot.transpose(1, 0, 2).reshape(GROUPS, OWN * PIECE)
        spot, place = lax.optimization_barrier((spot, place.reshape(tokens, 1)))
        results = attention(spot, received.reshape(N_SEQ * rows, 4 * DH), rows)
        returned = exchange(results.reshape(N_SEQ, rows, 4 * DH), "seq")
        key_rows = received[:, :, DH : 2 * DH].astype(jnp.float32).reshape(N_SEQ * rows, DH)
        squares = jnp.sum(key_rows * key_rows, axis=1)
        norm = jnp.sum(lax.all_gather(squares, "head"), axis=0)
        row = jnp.arange(rows, dtype=jnp.int32)[None, None, :] - here_start[:, :, None]
        held = (row >= 0) & (row < here_counts.astype(jnp.int32)[:, :, None])
        held = held.reshape(OWN, N_SEQ * rows)
        unit = jnp.where(held, 1.0 / jnp.sqrt(norm / D + EPSILON)[None], 0.0)
        means = jnp.dot(unit, key_rows, precision=lax.Precision.HIGHEST)
        means = means / jnp.sum(here_counts, axis=1)[:, None]
        spread = jnp.sum(means * means, axis=1, keepdims=True)
        spread = lax.optimization_barrier(jnp.broadcast_to(spread, (OWN, DH)))
        spread = jnp.sum(lax.all_gather(spread, "head"), axis=0)
        every, returned = seq_gather(means / jnp.sqrt(spread / D + EPSILON), returned)
        back = lax.rem(N_SEQ // 2 + seq // 2 - owner // 2, N_SEQ // 2)
        entry = back * 2 + ((owner ^ seq) & 1)
        centroids = every.reshape(CLUSTERS, DH)[entry * OWN + turn]
        outs = unpack(place, returned.reshape(N_SEQ * rows, 4 * DH))
        return (*outs, centroids)

    return lax.cond(
        most[0, 0] <= ROWS_SHORT,
        functools.partial(with_rows, ROWS_SHORT),
        functools.partial(with_rows, ROWS_FULL),
        queries,
        keys,
        values,
        d_out,
    )


def solution(mesh):
    wide = P("seq", "head")
    return jax.shard_map(
        body,
        mesh=mesh,
        in_specs=(wide, wide, wide, wide, P("seq", None)),
        out_specs=(wide, wide, wide, wide, P(None, "head")),
        check_vma=False,
    )
```

```python
import functools

import jax
import jax.numpy as jnp
from jax import lax
from jax.experimental import pallas as pl
from jax.experimental.pallas import tpu as pltpu
from jax.sharding import PartitionSpec as P

DH = 128
CLUSTERS = 256
CAPC = 12
D = 2048
N_SEQ = 32
OWN = CLUSTERS // N_SEQ
SLOTS = N_SEQ * CAPC
GROUP = 4
GROUPS = N_SEQ // GROUP
PIECE = GROUP * CAPC
ROWS_SHORT = 72
ROWS_FULL = OWN * CAPC
EPSILON = 1e-06
HIDDEN = 1e30
LOG2E = 1.4426950408889634
TOGETHER = 4
VMEM = 24 * 1024 * 1024
VMEM_MOST = 60 * 1024 * 1024


def iota(shape, dim):
    return lax.broadcasted_iota(jnp.int32, shape, dim)


def one_hot(mask):
    return jnp.where(mask, 1.0, 0.0).astype(jnp.bfloat16)


def dot(a, b, ca, cb):
    return lax.dot_general(a, b, (((ca,), (cb,)), ((), ())), preferred_element_type=jnp.float32)


def pack_kernel(
    rows, seq_ref, plan_ref, cluster_ref, ordinal_ref, q_ref, k_ref, v_ref, g_ref,
    out_ref, place_ref, all_ref, part_ref, sem_ref,
):
    step = pl.program_id(0)
    part = GROUP * rows

    @pl.when(step == 0)
    def _():
        for i, ref in enumerate((q_ref, k_ref, v_ref, g_ref)):
            all_ref[:, i * DH : (i + 1) * DH] = ref[...]
        chosen = (iota((N_SEQ, CLUSTERS), 0) == seq_ref[0, 0])
        start = jnp.sum(jnp.where(chosen, plan_ref[:N_SEQ], 0.0), axis=0, keepdims=True)
        owner = plan_ref[N_SEQ : N_SEQ + 1]
        table = jnp.where(iota((8, CLUSTERS), 0) == 0, owner, start).astype(jnp.bfloat16)
        tokens = cluster_ref.shape[1]
        member = one_hot(iota((CLUSTERS, tokens), 0) == cluster_ref[...])
        found = dot(table, member, 1, 0)
        place = found[0:1] * rows + found[1:2]
        place_ref[...] = place.astype(jnp.int32) + ordinal_ref[...]

    def copy(slot, at):
        return pltpu.make_async_copy(
            part_ref.at[slot], out_ref.at[pl.ds(pl.multiple_of(at * part, part), part)], sem_ref.at[slot]
        )

    slot = lax.rem(step, 2)

    @pl.when(step >= 2)
    def _():
        copy(slot, step - 2).wait()

    wanted = iota((part, place_ref.shape[1]), 0) + step * part
    part_ref[slot] = dot(one_hot(wanted == place_ref[...]), all_ref[...], 1, 0).astype(jnp.bfloat16)
    copy(slot, step).start()

    @pl.when(step == GROUPS - 1)
    def _():
        copy(1 - slot, step - 1).wait()
        copy(slot, step).wait()


def pack(seq, planned, cluster_row, ordinal_row, arrays, rows):
    tokens = cluster_row.shape[1]

    def whole(*shape):
        return pl.BlockSpec(shape, lambda i: (0, 0))

    return pl.pallas_call(
        functools.partial(pack_kernel, rows),
        grid=(GROUPS,),
        in_specs=[
            pl.BlockSpec(memory_space=pltpu.SMEM),
            whole(*planned.shape),
            whole(1, tokens),
            whole(1, tokens),
        ]
        + [whole(tokens, DH)] * 4,
        out_specs=[pl.BlockSpec(memory_space=pltpu.HBM), whole(1, tokens)],
        out_shape=[
            jax.ShapeDtypeStruct((N_SEQ * rows, 4 * DH), jnp.bfloat16),
            jax.ShapeDtypeStruct((1, tokens), jnp.int32),
        ],
        scratch_shapes=[
            pltpu.VMEM((tokens, 4 * DH), jnp.bfloat16),
            pltpu.VMEM((2, GROUP * rows, 4 * DH), jnp.bfloat16),
            pltpu.SemaphoreType.DMA((2,)),
        ],
        compiler_params=pltpu.CompilerParams(vmem_limit_bytes=VMEM_MOST),
        name="pack",
    )(seq, planned, cluster_row, ordinal_row, *arrays)


def unpack_kernel(place_ref, in_ref, *out_refs):
    tokens = place_ref.shape[0]
    chosen = one_hot(place_ref[...] == iota((tokens, in_ref.shape[0]), 1))
    rows = dot(chosen, in_ref[...], 1, 0).astype(jnp.bfloat16)
    for i, ref in enumerate(out_refs):
        ref[...] = rows[:, i * DH : (i + 1) * DH]


def unpack(place_column, block):
    tokens = place_column.shape[0]
    tile = 256
    return pl.pallas_call(
        unpack_kernel,
        grid=(tokens // tile,),
        in_specs=[
            pl.BlockSpec((tile, 1), lambda i: (i, 0)),
            pl.BlockSpec(block.shape, lambda i: (0, 0)),
        ],
        out_specs=[pl.BlockSpec((tile, DH), lambda i: (i, 0))] * 4,
        out_shape=[jax.ShapeDtypeStruct((tokens, DH), jnp.bfloat16)] * 4,
        compiler_params=pltpu.CompilerParams(vmem_limit_bytes=VMEM),
        name="unpack",
    )(place_column, block)


def attention_kernel(rows, place_ref, in_ref, out_ref, x_ref, hide_ref, y_ref):
    part = GROUP * rows
    scaling = DH**-0.5

    def chosen(g):
        return one_hot(iota((part, OWN * PIECE), 0) == place_ref[pl.ds(g, 1), :])

    def spread(g, _):
        block = in_ref[pl.ds(pl.multiple_of(g * part, part), part), :]
        block = jnp.concatenate([block, jnp.ones((part, DH), jnp.bfloat16)], axis=1)
        full = dot(chosen(g), block, 0, 0)
        moved = full[:, : 4 * DH].astype(jnp.bfloat16)
        hide = (full[:, 4 * DH :] - 1.0) * HIDDEN
        for k in range(OWN):
            at = pl.ds(pl.multiple_of(k * SLOTS + g * PIECE, 16), PIECE)
            x_ref[at, :] = moved[k * PIECE : (k + 1) * PIECE]
            hide_ref[at, :] = hide[k * PIECE : (k + 1) * PIECE]
        return 0

    lax.fori_loop(0, GROUPS, spread, 0)
    causal = iota((DH, DH), 0) <= iota((DH, DH), 1)

    def attend(k):
        at = pl.ds(pl.multiple_of(k * SLOTS, SLOTS), SLOTS)
        query, key = x_ref[at, 0:DH], x_ref[at, DH : 2 * DH]
        value, grad = x_ref[at, 2 * DH : 3 * DH], x_ref[at, 3 * DH : 4 * DH]
        hide = hide_ref[at, :]
        weights_all, changes_all = [], []
        for i in range(SLOTS // DH):
            low, high = i * DH, (i + 1) * DH
            scores = dot(key[:high], query[low:high], 1, 1) * (scaling * LOG2E) + hide[:high]
            last = jnp.where(causal, scores[low:], -HIDDEN)
            scores = last if i == 0 else jnp.concatenate([scores[:low], last], axis=0)
            weights = jnp.exp2(scores - jnp.max(scores, axis=0, keepdims=True))
            attention = weights * (1.0 / jnp.sum(weights, axis=0, keepdims=True))
            grad_weights = dot(value[:high], grad[low:high], 1, 1)
            delta = jnp.sum(attention * grad_weights, axis=0, keepdims=True)
            weights_all.append(attention.astype(jnp.bfloat16))
            changes_all.append((attention * (grad_weights - delta)).astype(jnp.bfloat16))
        outs, grad_queries = [], []
        for i in range(SLOTS // DH):
            high = (i + 1) * DH
            outs.append(dot(weights_all[i], value[:high], 0, 0))
            grad_queries.append(dot(changes_all[i], key[:high], 0, 0) * scaling)
        grad_values, grad_keys = [], []
        for j in range(SLOTS // DH):
            row = slice(j * DH, (j + 1) * DH)
            rest = slice(j * DH, SLOTS)
            wide = jnp.concatenate([w[row] for w in weights_all[j:]], axis=1)
            grad_values.append(dot(wide, grad[rest], 1, 0))
            wide = jnp.concatenate([c[row] for c in changes_all[j:]], axis=1)
            grad_keys.append(dot(wide, query[rest], 1, 0) * scaling)
        for i, pieces in enumerate((outs, grad_queries, grad_keys, grad_values)):
            y_ref[at, i * DH : (i + 1) * DH] = jnp.concatenate(pieces, axis=0).astype(jnp.bfloat16)

    def attend_several(i, _):
        for j in range(TOGETHER):
            attend(i * TOGETHER + j)
        return 0

    lax.fori_loop(0, OWN // TOGETHER, attend_several, 0)

    def gather(g, _):
        pieces = [
            y_ref[pl.ds(pl.multiple_of(k * SLOTS + g * PIECE, 16), PIECE), :] for k in range(OWN)
        ]
        block = dot(chosen(g), jnp.concatenate(pieces, axis=0), 1, 0)
        out_ref[pl.ds(pl.multiple_of(g * part, part), part), :] = block.astype(jnp.bfloat16)
        return 0

    lax.fori_loop(0, GROUPS, gather, 0)


def attention(places, block, rows):
    vmem = pl.BlockSpec(memory_space=pltpu.VMEM)
    return pl.pallas_call(
        functools.partial(attention_kernel, rows),
        in_specs=[vmem] * 2,
        out_specs=vmem,
        out_shape=jax.ShapeDtypeStruct(block.shape, jnp.bfloat16),
        scratch_shapes=[
            pltpu.VMEM((OWN * SLOTS, 4 * DH), jnp.bfloat16),
            pltpu.VMEM((OWN * SLOTS, DH), jnp.float32),
            pltpu.VMEM((OWN * SLOTS, 4 * DH), jnp.bfloat16),
        ],
        compiler_params=pltpu.CompilerParams(vmem_limit_bytes=VMEM),
        name="attention",
    )(places, block)


def across(x, step):
    low = (iota(x.shape, 1) & step) == 0
    return jnp.where(low, pltpu.roll(x, x.shape[1] - step, 1), pltpu.roll(x, step, 1))


def plan_kernel(counts_ref, out_ref, most_ref):
    counts = counts_ref[...]
    size_row = jnp.sum(counts, axis=0, keepdims=True)
    size_column = dot(counts.astype(jnp.bfloat16), jnp.ones((N_SEQ, CLUSTERS), jnp.bfloat16), 0, 0)
    square = (CLUSTERS, CLUSTERS)
    before = (size_column > size_row) | (
        (size_column == size_row) & (iota(square, 0) < iota(square, 1))
    )
    rank = jnp.sum(jnp.where(before, 1.0, 0.0), axis=0, keepdims=True).astype(jnp.int32)
    turn, spot = lax.shift_right_logical(rank, 5), rank & (N_SEQ - 1)
    owner = jnp.where((turn & 1) == 0, spot, N_SEQ - 1 - spot)
    number = iota((8, CLUSTERS), 1).astype(jnp.float32)
    named = jnp.concatenate([counts, number], axis=0).astype(jnp.bfloat16)
    tables = []
    for k in range(OWN):
        here = jnp.where(turn == k, owner, -1)
        tables.append(dot(named, one_hot(iota((DH, CLUSTERS), 0) == here), 1, 1))
    load = functools.reduce(jnp.add, [t[:N_SEQ] for t in tables])

    def cost(x):
        over = jnp.maximum(x - 60.0, 0.0)
        over = over * over
        return over * over

    for step in (1, 2, 4, 8, 16):
        other = across(load, step)
        for k in range(OWN):
            theirs = across(tables[k], step)
            change = theirs[:N_SEQ] - tables[k][:N_SEQ]
            more, less = load + change, other - change
            gain = (cost(more) + cost(less)) - (cost(load) + cost(other))
            swap = jnp.sum(gain, axis=0, keepdims=True) < 0.0
            load = jnp.where(swap, more, load)
            other = jnp.where(swap, less, other)
            tables[k] = jnp.where(swap, theirs, tables[k])
    owners = iota((N_SEQ, DH), 1)
    load = jnp.where(owners < N_SEQ, load, 0.0)
    most_ref[...] = jnp.max(jnp.max(load, axis=1, keepdims=True), axis=0, keepdims=True)
    start = jnp.zeros((N_SEQ, DH), jnp.float32)
    result = jnp.zeros((N_SEQ + 8, CLUSTERS), jnp.float32)
    for k in range(OWN):
        names = tables[k][N_SEQ : N_SEQ + 1]
        names = jnp.where(owners[:1] < N_SEQ, names, -1.0).astype(jnp.int32)
        extra = jnp.where(iota((8, DH), 0) == 0, iota((8, DH), 1), k).astype(jnp.float32)
        values = jnp.concatenate([start, extra], axis=0).astype(jnp.bfloat16)
        result += dot(values, one_hot(iota((CLUSTERS, DH), 0) == names), 1, 1)
        start = start + tables[k][:N_SEQ]
    out_ref[...] = result


def plan(counts):
    return pl.pallas_call(
        plan_kernel,
        out_shape=[
            jax.ShapeDtypeStruct((N_SEQ + 8, CLUSTERS), jnp.float32),
            jax.ShapeDtypeStruct((1, 1), jnp.float32),
        ],
        compiler_params=pltpu.CompilerParams(vmem_limit_bytes=VMEM),
        name="plan",
    )(counts)


def exchange(x, axis):
    return lax.all_to_all(x, axis, 0, 0, tiled=True)


def share(x, axis):
    return exchange(jnp.broadcast_to(x[None], (lax.axis_size(axis),) + x.shape), axis)


def seq_gather(x):
    swapped = lax.ppermute(x, "seq", [(i, i ^ 1) for i in range(N_SEQ)])
    x = jnp.stack([x, swapped])
    for stride in (1, 4):
        pieces = [x]
        for step in (1, 2, 3):
            away = 2 * stride * step
            pairs = [(i, (i + away) % N_SEQ) for i in range(N_SEQ)]
            pieces.append(lax.ppermute(x, "seq", pairs))
        if stride == 1:
            x = jnp.concatenate(pieces, axis=0)
    return pieces


def body(queries, keys, values, d_out, cluster_id):
    seq = lax.axis_index("seq")
    tokens = queries.shape[0]
    member = (cluster_id == iota((1, CLUSTERS), 1)).astype(jnp.int32)
    own_counts, cluster_id = lax.optimization_barrier((jnp.sum(member, axis=0), cluster_id))
    member = (cluster_id == iota((1, CLUSTERS), 1)).astype(jnp.int32)
    running = jnp.cumsum(member, axis=0)
    ordinal = jnp.sum((running - 1) * member, axis=1)
    counts = share(own_counts[None].astype(jnp.float32), "seq")[:, 0]
    counts, ordinal = lax.optimization_barrier((counts, ordinal))
    planned, most = plan(counts)

    def with_rows(rows, queries, keys, values, d_out):
        sent, place = pack(
            seq.reshape(1, 1),
            planned,
            cluster_id.reshape(1, tokens),
            ordinal.reshape(1, tokens),
            (queries, keys, values, d_out),
            rows,
        )
        received = exchange(sent.reshape(N_SEQ, rows, 4 * DH), "seq")
        plan_whole = planned.astype(jnp.int32)
        start, owner, turn = plan_whole[:N_SEQ], plan_whole[N_SEQ], plan_whole[N_SEQ + 1]
        turns = jnp.arange(OWN, dtype=jnp.int32)
        mine = (owner[None, :] == seq) & (turn[None, :] == turns[:, None])
        here_counts = jnp.sum(jnp.where(mine[:, None, :], counts[None], 0.0), axis=2)
        here_start = jnp.sum(jnp.where(mine[:, None, :], start[None], 0), axis=2)
        slot = jnp.arange(CAPC, dtype=jnp.int32)
        taken = slot[None, None, :] < here_counts.astype(jnp.int32)[:, :, None]
        line = (jnp.arange(N_SEQ, dtype=jnp.int32) % GROUP) * rows
        spot = here_start[:, :, None] + slot[None, None, :] + line[None, :, None]
        spot = jnp.where(taken, spot, -1).reshape(OWN, GROUPS, PIECE)
        spot = spot.transpose(1, 0, 2).reshape(GROUPS, OWN * PIECE)
        spot, place = lax.optimization_barrier((spot, place.reshape(tokens, 1)))
        results = attention(spot, received.reshape(N_SEQ * rows, 4 * DH), rows)
        returned = exchange(results.reshape(N_SEQ, rows, 4 * DH), "seq")
        key_rows = received[:, :, DH : 2 * DH].astype(jnp.float32).reshape(N_SEQ * rows, DH)
        squares = jnp.sum(key_rows * key_rows, axis=1)
        norm = jnp.sum(lax.all_gather(squares, "head"), axis=0)
        row = jnp.arange(rows, dtype=jnp.int32)[None, None, :] - here_start[:, :, None]
        held = (row >= 0) & (row < here_counts.astype(jnp.int32)[:, :, None])
        held = held.reshape(OWN, N_SEQ * rows)
        unit = jnp.where(held, 1.0 / jnp.sqrt(norm / D + EPSILON)[None], 0.0)
        means = jnp.dot(unit, key_rows, precision=lax.Precision.HIGHEST)
        means = means / jnp.sum(here_counts, axis=1)[:, None]
        spread = jnp.sum(means * means, axis=1, keepdims=True)
        spread = lax.optimization_barrier(jnp.broadcast_to(spread, (OWN, DH)))
        spread = jnp.sum(lax.all_gather(spread, "head"), axis=0)
        pieces = seq_gather(means / jnp.sqrt(spread / D + EPSILON))
        back = lax.rem(N_SEQ // 2 + seq // 2 - owner // 2, N_SEQ // 2)
        entry = back * 2 + ((owner ^ seq) & 1)
        outs = unpack(place, returned.reshape(N_SEQ * rows, 4 * DH))
        pieces, outs = lax.optimization_barrier((pieces, outs))
        every = jnp.concatenate(pieces, axis=0).reshape(CLUSTERS, DH)
        centroids = every[entry * OWN + turn]
        return (*outs, centroids)

    return lax.cond(
        most[0, 0] <= ROWS_SHORT,
        functools.partial(with_rows, ROWS_SHORT),
        functools.partial(with_rows, ROWS_FULL),
        queries,
        keys,
        values,
        d_out,
    )


def solution(mesh):
    wide = P("seq", "head")
    return jax.shard_map(
        body,
        mesh=mesh,
        in_specs=(wide, wide, wide, wide, P("seq", None)),
        out_specs=(wide, wide, wide, wide, P(None, "head")),
        check_vma=False,
    )
```

```python
import functools

import jax
import jax.numpy as jnp
from jax import lax
from jax.experimental import pallas as pl
from jax.experimental.pallas import tpu as pltpu
from jax.sharding import PartitionSpec as P

DH = 128
CLUSTERS = 256
CAPC = 12
D = 2048
N_SEQ = 32
OWN = CLUSTERS // N_SEQ
SLOTS = N_SEQ * CAPC
GROUP = 4
GROUPS = N_SEQ // GROUP
PIECE = GROUP * CAPC
ROWS_SHORT = 72
ROWS_FULL = OWN * CAPC
EPSILON = 1e-06
NEAR = 6
HIDDEN = 1e30
LOG2E = 1.4426950408889634
TOGETHER = 4
VMEM = 24 * 1024 * 1024
VMEM_MOST = 60 * 1024 * 1024


def iota(shape, dim):
    return lax.broadcasted_iota(jnp.int32, shape, dim)


def one_hot(mask):
    return jnp.where(mask, 1.0, 0.0).astype(jnp.bfloat16)


def dot(a, b, ca, cb):
    return lax.dot_general(a, b, (((ca,), (cb,)), ((), ())), preferred_element_type=jnp.float32)


def pack_kernel(
    rows, seq_ref, plan_ref, cluster_ref, ordinal_ref, q_ref, k_ref, v_ref, g_ref,
    out_ref, place_ref, all_ref, part_ref, sem_ref,
):
    step = pl.program_id(0)
    part = GROUP * rows

    @pl.when(step == 0)
    def _():
        for i, ref in enumerate((q_ref, k_ref, v_ref, g_ref)):
            all_ref[:, i * DH : (i + 1) * DH] = ref[...]
        chosen = (iota((N_SEQ, CLUSTERS), 0) == seq_ref[0, 0])
        start = jnp.sum(jnp.where(chosen, plan_ref[:N_SEQ], 0.0), axis=0, keepdims=True)
        owner = plan_ref[N_SEQ : N_SEQ + 1]
        table = jnp.where(iota((8, CLUSTERS), 0) == 0, owner, start).astype(jnp.bfloat16)
        tokens = cluster_ref.shape[1]
        member = one_hot(iota((CLUSTERS, tokens), 0) == cluster_ref[...])
        found = dot(table, member, 1, 0)
        place = found[0:1] * rows + found[1:2]
        place_ref[...] = place.astype(jnp.int32) + ordinal_ref[...]

    def copy(slot, at):
        return pltpu.make_async_copy(
            part_ref.at[slot], out_ref.at[pl.ds(pl.multiple_of(at * part, part), part)], sem_ref.at[slot]
        )

    slot = lax.rem(step, 2)

    @pl.when(step >= 2)
    def _():
        copy(slot, step - 2).wait()

    wanted = iota((part, place_ref.shape[1]), 0) + step * part
    part_ref[slot] = dot(one_hot(wanted == place_ref[...]), all_ref[...], 1, 0).astype(jnp.bfloat16)
    copy(slot, step).start()

    @pl.when(step == GROUPS - 1)
    def _():
        copy(1 - slot, step - 1).wait()
        copy(slot, step).wait()


def pack(seq, planned, cluster_row, ordinal_row, arrays, rows):
    tokens = cluster_row.shape[1]

    def whole(*shape):
        return pl.BlockSpec(shape, lambda i: (0, 0))

    return pl.pallas_call(
        functools.partial(pack_kernel, rows),
        grid=(GROUPS,),
        in_specs=[
            pl.BlockSpec(memory_space=pltpu.SMEM),
            whole(*planned.shape),
            whole(1, tokens),
            whole(1, tokens),
        ]
        + [whole(tokens, DH)] * 4,
        out_specs=[pl.BlockSpec(memory_space=pltpu.HBM), whole(1, tokens)],
        out_shape=[
            jax.ShapeDtypeStruct((N_SEQ * rows, 4 * DH), jnp.bfloat16),
            jax.ShapeDtypeStruct((1, tokens), jnp.int32),
        ],
        scratch_shapes=[
            pltpu.VMEM((tokens, 4 * DH), jnp.bfloat16),
            pltpu.VMEM((2, GROUP * rows, 4 * DH), jnp.bfloat16),
            pltpu.SemaphoreType.DMA((2,)),
        ],
        compiler_params=pltpu.CompilerParams(vmem_limit_bytes=VMEM_MOST),
        name="pack",
    )(seq, planned, cluster_row, ordinal_row, *arrays)


def unpack_kernel(place_ref, in_ref, *out_refs):
    tokens = place_ref.shape[0]
    chosen = one_hot(place_ref[...] == iota((tokens, in_ref.shape[0]), 1))
    rows = dot(chosen, in_ref[...], 1, 0).astype(jnp.bfloat16)
    for i, ref in enumerate(out_refs):
        ref[...] = rows[:, i * DH : (i + 1) * DH]


def unpack(place_column, block):
    tokens = place_column.shape[0]
    tile = 256
    return pl.pallas_call(
        unpack_kernel,
        grid=(tokens // tile,),
        in_specs=[
            pl.BlockSpec((tile, 1), lambda i: (i, 0)),
            pl.BlockSpec(block.shape, lambda i: (0, 0)),
        ],
        out_specs=[pl.BlockSpec((tile, DH), lambda i: (i, 0))] * 4,
        out_shape=[jax.ShapeDtypeStruct((tokens, DH), jnp.bfloat16)] * 4,
        compiler_params=pltpu.CompilerParams(vmem_limit_bytes=VMEM),
        name="unpack",
    )(place_column, block)


def attention_kernel(rows, place_ref, in_ref, out_ref, x_ref, hide_ref, y_ref):
    part = GROUP * rows
    scaling = DH**-0.5

    def chosen(g):
        return one_hot(iota((part, OWN * PIECE), 0) == place_ref[pl.ds(g, 1), :])

    def spread(g, _):
        block = in_ref[pl.ds(pl.multiple_of(g * part, part), part), :]
        block = jnp.concatenate([block, jnp.ones((part, DH), jnp.bfloat16)], axis=1)
        full = dot(chosen(g), block, 0, 0)
        moved = full[:, : 4 * DH].astype(jnp.bfloat16)
        hide = (full[:, 4 * DH :] - 1.0) * HIDDEN
        for k in range(OWN):
            at = pl.ds(pl.multiple_of(k * SLOTS + g * PIECE, 16), PIECE)
            x_ref[at, :] = moved[k * PIECE : (k + 1) * PIECE]
            hide_ref[at, :] = hide[k * PIECE : (k + 1) * PIECE]
        return 0

    lax.fori_loop(0, GROUPS, spread, 0)
    causal = iota((DH, DH), 0) <= iota((DH, DH), 1)

    def attend(k):
        at = pl.ds(pl.multiple_of(k * SLOTS, SLOTS), SLOTS)
        query, key = x_ref[at, 0:DH], x_ref[at, DH : 2 * DH]
        value, grad = x_ref[at, 2 * DH : 3 * DH], x_ref[at, 3 * DH : 4 * DH]
        hide = hide_ref[at, :]
        weights_all, changes_all = [], []
        for i in range(SLOTS // DH):
            low, high = i * DH, (i + 1) * DH
            scores = dot(key[:high], query[low:high], 1, 1) * (scaling * LOG2E) + hide[:high]
            last = jnp.where(causal, scores[low:], -HIDDEN)
            scores = last if i == 0 else jnp.concatenate([scores[:low], last], axis=0)
            weights = jnp.exp2(scores - jnp.max(scores, axis=0, keepdims=True))
            attention = weights * (1.0 / jnp.sum(weights, axis=0, keepdims=True))
            grad_weights = dot(value[:high], grad[low:high], 1, 1)
            delta = jnp.sum(attention * grad_weights, axis=0, keepdims=True)
            weights_all.append(attention.astype(jnp.bfloat16))
            changes_all.append((attention * (grad_weights - delta)).astype(jnp.bfloat16))
        outs, grad_queries = [], []
        for i in range(SLOTS // DH):
            high = (i + 1) * DH
            outs.append(dot(weights_all[i], value[:high], 0, 0))
            grad_queries.append(dot(changes_all[i], key[:high], 0, 0) * scaling)
        grad_values, grad_keys = [], []
        for j in range(SLOTS // DH):
            row = slice(j * DH, (j + 1) * DH)
            rest = slice(j * DH, SLOTS)
            wide = jnp.concatenate([w[row] for w in weights_all[j:]], axis=1)
            grad_values.append(dot(wide, grad[rest], 1, 0))
            wide = jnp.concatenate([c[row] for c in changes_all[j:]], axis=1)
            grad_keys.append(dot(wide, query[rest], 1, 0) * scaling)
        for i, pieces in enumerate((outs, grad_queries, grad_keys, grad_values)):
            y_ref[at, i * DH : (i + 1) * DH] = jnp.concatenate(pieces, axis=0).astype(jnp.bfloat16)

    def attend_several(i, _):
        for j in range(TOGETHER):
            attend(i * TOGETHER + j)
        return 0

    lax.fori_loop(0, OWN // TOGETHER, attend_several, 0)

    def gather(g, _):
        pieces = [
            y_ref[pl.ds(pl.multiple_of(k * SLOTS + g * PIECE, 16), PIECE), :] for k in range(OWN)
        ]
        block = dot(chosen(g), jnp.concatenate(pieces, axis=0), 1, 0)
        out_ref[pl.ds(pl.multiple_of(g * part, part), part), :] = block.astype(jnp.bfloat16)
        return 0

    lax.fori_loop(0, GROUPS, gather, 0)


def attention(places, block, rows):
    vmem = pl.BlockSpec(memory_space=pltpu.VMEM)
    return pl.pallas_call(
        functools.partial(attention_kernel, rows),
        in_specs=[vmem] * 2,
        out_specs=vmem,
        out_shape=jax.ShapeDtypeStruct(block.shape, jnp.bfloat16),
        scratch_shapes=[
            pltpu.VMEM((OWN * SLOTS, 4 * DH), jnp.bfloat16),
            pltpu.VMEM((OWN * SLOTS, DH), jnp.float32),
            pltpu.VMEM((OWN * SLOTS, 4 * DH), jnp.bfloat16),
        ],
        compiler_params=pltpu.CompilerParams(vmem_limit_bytes=VMEM),
        name="attention",
    )(places, block)


def across(x, step):
    low = (iota(x.shape, 1) & step) == 0
    return jnp.where(low, pltpu.roll(x, x.shape[1] - step, 1), pltpu.roll(x, step, 1))


def plan_kernel(counts_ref, out_ref, most_ref):
    counts = counts_ref[...]
    size_row = jnp.sum(counts, axis=0, keepdims=True)
    size_column = dot(counts.astype(jnp.bfloat16), jnp.ones((N_SEQ, CLUSTERS), jnp.bfloat16), 0, 0)
    square = (CLUSTERS, CLUSTERS)
    before = (size_column > size_row) | (
        (size_column == size_row) & (iota(square, 0) < iota(square, 1))
    )
    rank = jnp.sum(jnp.where(before, 1.0, 0.0), axis=0, keepdims=True).astype(jnp.int32)
    turn, spot = lax.shift_right_logical(rank, 5), rank & (N_SEQ - 1)
    owner = jnp.where((turn & 1) == 0, spot, N_SEQ - 1 - spot)
    number = iota((8, CLUSTERS), 1).astype(jnp.float32)
    named = jnp.concatenate([counts, number], axis=0).astype(jnp.bfloat16)
    tables = []
    for k in range(OWN):
        here = jnp.where(turn == k, owner, -1)
        tables.append(dot(named, one_hot(iota((DH, CLUSTERS), 0) == here), 1, 1))
    load = functools.reduce(jnp.add, [t[:N_SEQ] for t in tables])

    def cost(x):
        over = jnp.maximum(x - 60.0, 0.0)
        over = over * over
        return over * over

    for step in (1, 2, 4, 8, 16):
        other = across(load, step)
        for k in range(OWN):
            theirs = across(tables[k], step)
            change = theirs[:N_SEQ] - tables[k][:N_SEQ]
            more, less = load + change, other - change
            gain = (cost(more) + cost(less)) - (cost(load) + cost(other))
            swap = jnp.sum(gain, axis=0, keepdims=True) < 0.0
            load = jnp.where(swap, more, load)
            other = jnp.where(swap, less, other)
            tables[k] = jnp.where(swap, theirs, tables[k])
    owners = iota((N_SEQ, DH), 1)
    load = jnp.where(owners < N_SEQ, load, 0.0)
    most_ref[...] = jnp.max(jnp.max(load, axis=1, keepdims=True), axis=0, keepdims=True)
    start = jnp.zeros((N_SEQ, DH), jnp.float32)
    result = jnp.zeros((N_SEQ + 8, CLUSTERS), jnp.float32)
    for k in range(OWN):
        names = tables[k][N_SEQ : N_SEQ + 1]
        names = jnp.where(owners[:1] < N_SEQ, names, -1.0).astype(jnp.int32)
        extra = jnp.where(iota((8, DH), 0) == 0, iota((8, DH), 1), k).astype(jnp.float32)
        values = jnp.concatenate([start, extra], axis=0).astype(jnp.bfloat16)
        result += dot(values, one_hot(iota((CLUSTERS, DH), 0) == names), 1, 1)
        start = start + tables[k][:N_SEQ]
    out_ref[...] = result


def plan(counts):
    return pl.pallas_call(
        plan_kernel,
        out_shape=[
            jax.ShapeDtypeStruct((N_SEQ + 8, CLUSTERS), jnp.float32),
            jax.ShapeDtypeStruct((1, 1), jnp.float32),
        ],
        compiler_params=pltpu.CompilerParams(vmem_limit_bytes=VMEM),
        name="plan",
    )(counts)


def exchange(x, axis):
    return lax.all_to_all(x, axis, 0, 0, tiled=True)


def share(x, axis):
    return exchange(jnp.broadcast_to(x[None], (lax.axis_size(axis),) + x.shape), axis)


def seq_gather(x):
    swapped = lax.ppermute(x, "seq", [(i, i ^ 1) for i in range(N_SEQ)])
    x = jnp.stack([x, swapped])
    pieces = [x]
    for step in range(1, NEAR):
        pieces.append(far(x, step))
    return jnp.concatenate(pieces, axis=0)


def far(x, chips):
    return lax.ppermute(x, "seq", [(i, (i + 2 * chips) % N_SEQ) for i in range(N_SEQ)])


def body(queries, keys, values, d_out, cluster_id):
    seq = lax.axis_index("seq")
    tokens = queries.shape[0]
    member = (cluster_id == iota((1, CLUSTERS), 1)).astype(jnp.int32)
    own_counts, cluster_id = lax.optimization_barrier((jnp.sum(member, axis=0), cluster_id))
    member = (cluster_id == iota((1, CLUSTERS), 1)).astype(jnp.int32)
    running = jnp.cumsum(member, axis=0)
    ordinal = jnp.sum((running - 1) * member, axis=1)
    counts = share(own_counts[None].astype(jnp.float32), "seq")[:, 0]
    counts, ordinal = lax.optimization_barrier((counts, ordinal))
    planned, most = plan(counts)

    def with_rows(rows, queries, keys, values, d_out):
        sent, place = pack(
            seq.reshape(1, 1),
            planned,
            cluster_id.reshape(1, tokens),
            ordinal.reshape(1, tokens),
            (queries, keys, values, d_out),
            rows,
        )
        received = exchange(sent.reshape(N_SEQ, rows, 4 * DH), "seq")
        plan_whole = planned.astype(jnp.int32)
        start, owner, turn = plan_whole[:N_SEQ], plan_whole[N_SEQ], plan_whole[N_SEQ + 1]
        turns = jnp.arange(OWN, dtype=jnp.int32)
        mine = (owner[None, :] == seq) & (turn[None, :] == turns[:, None])
        here_counts = jnp.sum(jnp.where(mine[:, None, :], counts[None], 0.0), axis=2)
        here_start = jnp.sum(jnp.where(mine[:, None, :], start[None], 0), axis=2)
        slot = jnp.arange(CAPC, dtype=jnp.int32)
        taken = slot[None, None, :] < here_counts.astype(jnp.int32)[:, :, None]
        line = (jnp.arange(N_SEQ, dtype=jnp.int32) % GROUP) * rows
        spot = here_start[:, :, None] + slot[None, None, :] + line[None, :, None]
        spot = jnp.where(taken, spot, -1).reshape(OWN, GROUPS, PIECE)
        spot = spot.transpose(1, 0, 2).reshape(GROUPS, OWN * PIECE)
        spot, place = lax.optimization_barrier((spot, place.reshape(tokens, 1)))
        results = attention(spot, received.reshape(N_SEQ * rows, 4 * DH), rows)
        results, keys_in = lax.optimization_barrier((results, received[:, :, DH : 2 * DH]))
        returned = exchange(results.reshape(N_SEQ, rows, 4 * DH), "seq")
        key_rows = keys_in.astype(jnp.float32).reshape(N_SEQ * rows, DH)
        squares = jnp.sum(key_rows * key_rows, axis=1)
        norm = jnp.sum(lax.all_gather(squares, "head"), axis=0)
        row = jnp.arange(rows, dtype=jnp.int32)[None, None, :] - here_start[:, :, None]
        held = (row >= 0) & (row < here_counts.astype(jnp.int32)[:, :, None])
        held = held.reshape(OWN, N_SEQ * rows)
        unit = jnp.where(held, 1.0 / jnp.sqrt(norm / D + EPSILON)[None], 0.0)
        means = jnp.dot(unit, key_rows, precision=lax.Precision.HIGHEST)
        means = means / jnp.sum(here_counts, axis=1)[:, None]
        spread = jnp.sum(means * means, axis=1, keepdims=True)
        spread = lax.optimization_barrier(jnp.broadcast_to(spread, (OWN, DH)))
        spread = jnp.sum(lax.all_gather(spread, "head"), axis=0)
        near = seq_gather(means / jnp.sqrt(spread / D + EPSILON))
        back = lax.rem(N_SEQ // 2 + seq // 2 - owner // 2, N_SEQ // 2)
        entry = back * 2 + ((owner ^ seq) & 1)
        outs = unpack(place, returned.reshape(N_SEQ * rows, 4 * DH))
        near, outs = lax.optimization_barrier((near, outs))
        pieces = [near] + [far(near, step) for step in range(NEAR, N_SEQ // 2, NEAR)]
        every = jnp.concatenate(pieces, axis=0).reshape(-1, DH)
        centroids = every[entry * OWN + turn]
        return (*outs, centroids)

    return lax.cond(
        most[0, 0] <= ROWS_SHORT,
        functools.partial(with_rows, ROWS_SHORT),
        functools.partial(with_rows, ROWS_FULL),
        queries,
        keys,
        values,
        d_out,
    )


def solution(mesh):
    wide = P("seq", "head")
    return jax.shard_map(
        body,
        mesh=mesh,
        in_specs=(wide, wide, wide, wide, P("seq", None)),
        out_specs=(wide, wide, wide, wide, P(None, "head")),
        check_vma=False,
    )
```

```python
import functools

import jax
import jax.numpy as jnp
from jax import lax
from jax.experimental import pallas as pl
from jax.experimental.pallas import tpu as pltpu
from jax.sharding import PartitionSpec as P

DH = 128
CLUSTERS = 256
CAPC = 12
D = 2048
N_SEQ = 32
OWN = CLUSTERS // N_SEQ
SLOTS = N_SEQ * CAPC
GROUP = 4
GROUPS = N_SEQ // GROUP
PIECE = GROUP * CAPC
ROWS_SHORT = 72
ROWS_FULL = OWN * CAPC
EPSILON = 1e-06
NEAR = 6
HIDDEN = 1e30
LOG2E = 1.4426950408889634
SIDE_BY_SIDE = 4
TOGETHER = 4
VMEM = 24 * 1024 * 1024
VMEM_MOST = 60 * 1024 * 1024


def iota(shape, dim):
    return lax.broadcasted_iota(jnp.int32, shape, dim)


def one_hot(mask):
    return jnp.where(mask, 1.0, 0.0).astype(jnp.bfloat16)


def dot(a, b, ca, cb):
    return lax.dot_general(a, b, (((ca,), (cb,)), ((), ())), preferred_element_type=jnp.float32)


def pack_kernel(
    rows, seq_ref, plan_ref, cluster_ref, ordinal_ref, q_ref, k_ref, v_ref, g_ref,
    out_ref, place_ref, all_ref, part_ref, sem_ref,
):
    step = pl.program_id(0)
    part = GROUP * rows

    @pl.when(step == 0)
    def _():
        for i, ref in enumerate((q_ref, k_ref, v_ref, g_ref)):
            all_ref[:, i * DH : (i + 1) * DH] = ref[...]
        chosen = (iota((N_SEQ, CLUSTERS), 0) == seq_ref[0, 0])
        start = jnp.sum(jnp.where(chosen, plan_ref[:N_SEQ], 0.0), axis=0, keepdims=True)
        owner = plan_ref[N_SEQ : N_SEQ + 1]
        table = jnp.where(iota((8, CLUSTERS), 0) == 0, owner, start).astype(jnp.bfloat16)
        tokens = cluster_ref.shape[1]
        member = one_hot(iota((CLUSTERS, tokens), 0) == cluster_ref[...])
        found = dot(table, member, 1, 0)
        place = found[0:1] * rows + found[1:2]
        place_ref[...] = place.astype(jnp.int32) + ordinal_ref[...]

    def copy(slot, at):
        return pltpu.make_async_copy(
            part_ref.at[slot], out_ref.at[pl.ds(pl.multiple_of(at * part, part), part)], sem_ref.at[slot]
        )

    slot = lax.rem(step, 2)

    @pl.when(step >= 2)
    def _():
        copy(slot, step - 2).wait()

    wanted = iota((part, place_ref.shape[1]), 0) + step * part
    part_ref[slot] = dot(one_hot(wanted == place_ref[...]), all_ref[...], 1, 0).astype(jnp.bfloat16)
    copy(slot, step).start()

    @pl.when(step == GROUPS - 1)
    def _():
        copy(1 - slot, step - 1).wait()
        copy(slot, step).wait()


def pack(seq, planned, cluster_row, ordinal_row, arrays, rows):
    tokens = cluster_row.shape[1]

    def whole(*shape):
        return pl.BlockSpec(shape, lambda i: (0, 0))

    return pl.pallas_call(
        functools.partial(pack_kernel, rows),
        grid=(GROUPS,),
        in_specs=[
            pl.BlockSpec(memory_space=pltpu.SMEM),
            whole(*planned.shape),
            whole(1, tokens),
            whole(1, tokens),
        ]
        + [whole(tokens, DH)] * 4,
        out_specs=[pl.BlockSpec(memory_space=pltpu.HBM), whole(1, tokens)],
        out_shape=[
            jax.ShapeDtypeStruct((N_SEQ * rows, 4 * DH), jnp.bfloat16),
            jax.ShapeDtypeStruct((1, tokens), jnp.int32),
        ],
        scratch_shapes=[
            pltpu.VMEM((tokens, 4 * DH), jnp.bfloat16),
            pltpu.VMEM((2, GROUP * rows, 4 * DH), jnp.bfloat16),
            pltpu.SemaphoreType.DMA((2,)),
        ],
        compiler_params=pltpu.CompilerParams(vmem_limit_bytes=VMEM_MOST),
        name="pack",
    )(seq, planned, cluster_row, ordinal_row, *arrays)


def unpack_kernel(place_ref, in_ref, *out_refs):
    tokens = place_ref.shape[0]
    chosen = one_hot(place_ref[...] == iota((tokens, in_ref.shape[0]), 1))
    rows = dot(chosen, in_ref[...], 1, 0).astype(jnp.bfloat16)
    for i, ref in enumerate(out_refs):
        ref[...] = rows[:, i * DH : (i + 1) * DH]


def unpack(place_column, block):
    tokens = place_column.shape[0]
    tile = 512
    return pl.pallas_call(
        unpack_kernel,
        grid=(tokens // tile,),
        in_specs=[
            pl.BlockSpec((tile, 1), lambda i: (i, 0)),
            pl.BlockSpec(block.shape, lambda i: (0, 0)),
        ],
        out_specs=[pl.BlockSpec((tile, DH), lambda i: (i, 0))] * 4,
        out_shape=[jax.ShapeDtypeStruct((tokens, DH), jnp.bfloat16)] * 4,
        compiler_params=pltpu.CompilerParams(vmem_limit_bytes=VMEM),
        name="unpack",
    )(place_column, block)


def attention_kernel(rows, place_ref, in_ref, out_ref, x_ref, hide_ref, y_ref):
    part = GROUP * rows
    scaling = DH**-0.5

    def chosen(g):
        return one_hot(iota((part, OWN * PIECE), 0) == place_ref[pl.ds(g, 1), :])

    def several(work):
        def one(i, _):
            for j in range(SIDE_BY_SIDE):
                work(i * SIDE_BY_SIDE + j, 0)
            return 0

        return one

    def spread(g, _):
        block = in_ref[pl.ds(pl.multiple_of(g * part, part), part), :]
        block = jnp.concatenate([block, jnp.ones((part, DH), jnp.bfloat16)], axis=1)
        full = dot(chosen(g), block, 0, 0)
        moved = full[:, : 4 * DH].astype(jnp.bfloat16)
        hide = (full[:, 4 * DH :] - 1.0) * HIDDEN
        for k in range(OWN):
            at = pl.ds(pl.multiple_of(k * SLOTS + g * PIECE, 16), PIECE)
            x_ref[at, :] = moved[k * PIECE : (k + 1) * PIECE]
            hide_ref[at, :] = hide[k * PIECE : (k + 1) * PIECE]
        return 0

    lax.fori_loop(0, GROUPS // SIDE_BY_SIDE, several(spread), 0)
    causal = iota((DH, DH), 0) <= iota((DH, DH), 1)

    def attend(k):
        at = pl.ds(pl.multiple_of(k * SLOTS, SLOTS), SLOTS)
        query, key = x_ref[at, 0:DH], x_ref[at, DH : 2 * DH]
        value, grad = x_ref[at, 2 * DH : 3 * DH], x_ref[at, 3 * DH : 4 * DH]
        hide = hide_ref[at, :]
        weights_all, changes_all = [], []
        for i in range(SLOTS // DH):
            low, high = i * DH, (i + 1) * DH
            scores = dot(key[:high], query[low:high], 1, 1) * (scaling * LOG2E) + hide[:high]
            last = jnp.where(causal, scores[low:], -HIDDEN)
            scores = last if i == 0 else jnp.concatenate([scores[:low], last], axis=0)
            weights = jnp.exp2(scores - jnp.max(scores, axis=0, keepdims=True))
            attention = weights * (1.0 / jnp.sum(weights, axis=0, keepdims=True))
            grad_weights = dot(value[:high], grad[low:high], 1, 1)
            delta = jnp.sum(attention * grad_weights, axis=0, keepdims=True)
            weights_all.append(attention.astype(jnp.bfloat16))
            changes_all.append((attention * (grad_weights - delta)).astype(jnp.bfloat16))
        outs, grad_queries = [], []
        for i in range(SLOTS // DH):
            high = (i + 1) * DH
            outs.append(dot(weights_all[i], value[:high], 0, 0))
            grad_queries.append(dot(changes_all[i], key[:high], 0, 0) * scaling)
        grad_values, grad_keys = [], []
        for j in range(SLOTS // DH):
            row = slice(j * DH, (j + 1) * DH)
            rest = slice(j * DH, SLOTS)
            wide = jnp.concatenate([w[row] for w in weights_all[j:]], axis=1)
            grad_values.append(dot(wide, grad[rest], 1, 0))
            wide = jnp.concatenate([c[row] for c in changes_all[j:]], axis=1)
            grad_keys.append(dot(wide, query[rest], 1, 0) * scaling)
        for i, pieces in enumerate((outs, grad_queries, grad_keys, grad_values)):
            y_ref[at, i * DH : (i + 1) * DH] = jnp.concatenate(pieces, axis=0).astype(jnp.bfloat16)

    def attend_several(i, _):
        for j in range(TOGETHER):
            attend(i * TOGETHER + j)
        return 0

    lax.fori_loop(0, OWN // TOGETHER, attend_several, 0)

    def gather(g, _):
        pieces = [
            y_ref[pl.ds(pl.multiple_of(k * SLOTS + g * PIECE, 16), PIECE), :] for k in range(OWN)
        ]
        block = dot(chosen(g), jnp.concatenate(pieces, axis=0), 1, 0)
        out_ref[pl.ds(pl.multiple_of(g * part, part), part), :] = block.astype(jnp.bfloat16)
        return 0

    lax.fori_loop(0, GROUPS // SIDE_BY_SIDE, several(gather), 0)


def attention(places, block, rows):
    vmem = pl.BlockSpec(memory_space=pltpu.VMEM)
    return pl.pallas_call(
        functools.partial(attention_kernel, rows),
        in_specs=[vmem] * 2,
        out_specs=vmem,
        out_shape=jax.ShapeDtypeStruct(block.shape, jnp.bfloat16),
        scratch_shapes=[
            pltpu.VMEM((OWN * SLOTS, 4 * DH), jnp.bfloat16),
            pltpu.VMEM((OWN * SLOTS, DH), jnp.float32),
            pltpu.VMEM((OWN * SLOTS, 4 * DH), jnp.bfloat16),
        ],
        compiler_params=pltpu.CompilerParams(vmem_limit_bytes=VMEM),
        name="attention",
    )(places, block)


def across(x, step):
    low = (iota(x.shape, 1) & step) == 0
    return jnp.where(low, pltpu.roll(x, x.shape[1] - step, 1), pltpu.roll(x, step, 1))


def plan_kernel(counts_ref, out_ref, most_ref):
    counts = counts_ref[...]
    size_row = jnp.sum(counts, axis=0, keepdims=True)
    size_column = dot(counts.astype(jnp.bfloat16), jnp.ones((N_SEQ, CLUSTERS), jnp.bfloat16), 0, 0)
    square = (CLUSTERS, CLUSTERS)
    before = (size_column > size_row) | (
        (size_column == size_row) & (iota(square, 0) < iota(square, 1))
    )
    rank = jnp.sum(jnp.where(before, 1.0, 0.0), axis=0, keepdims=True).astype(jnp.int32)
    turn, spot = lax.shift_right_logical(rank, 5), rank & (N_SEQ - 1)
    owner = jnp.where((turn & 1) == 0, spot, N_SEQ - 1 - spot)
    number = iota((8, CLUSTERS), 1).astype(jnp.float32)
    named = jnp.concatenate([counts, number], axis=0).astype(jnp.bfloat16)
    tables = []
    for k in range(OWN):
        here = jnp.where(turn == k, owner, -1)
        tables.append(dot(named, one_hot(iota((DH, CLUSTERS), 0) == here), 1, 1))
    load = functools.reduce(jnp.add, [t[:N_SEQ] for t in tables])

    def cost(x):
        over = jnp.maximum(x - 60.0, 0.0)
        over = over * over
        return over * over

    for step in (1, 2, 4, 8, 16):
        other = across(load, step)
        for k in range(OWN):
            theirs = across(tables[k], step)
            change = theirs[:N_SEQ] - tables[k][:N_SEQ]
            more, less = load + change, other - change
            gain = (cost(more) + cost(less)) - (cost(load) + cost(other))
            swap = jnp.sum(gain, axis=0, keepdims=True) < 0.0
            load = jnp.where(swap, more, load)
            other = jnp.where(swap, less, other)
            tables[k] = jnp.where(swap, theirs, tables[k])
    owners = iota((N_SEQ, DH), 1)
    load = jnp.where(owners < N_SEQ, load, 0.0)
    most_ref[...] = jnp.max(jnp.max(load, axis=1, keepdims=True), axis=0, keepdims=True)
    start = jnp.zeros((N_SEQ, DH), jnp.float32)
    result = jnp.zeros((N_SEQ + 8, CLUSTERS), jnp.float32)
    for k in range(OWN):
        names = tables[k][N_SEQ : N_SEQ + 1]
        names = jnp.where(owners[:1] < N_SEQ, names, -1.0).astype(jnp.int32)
        extra = jnp.where(iota((8, DH), 0) == 0, iota((8, DH), 1), k).astype(jnp.float32)
        values = jnp.concatenate([start, extra], axis=0).astype(jnp.bfloat16)
        result += dot(values, one_hot(iota((CLUSTERS, DH), 0) == names), 1, 1)
        start = start + tables[k][:N_SEQ]
    out_ref[...] = result


def plan(counts):
    return pl.pallas_call(
        plan_kernel,
        out_shape=[
            jax.ShapeDtypeStruct((N_SEQ + 8, CLUSTERS), jnp.float32),
            jax.ShapeDtypeStruct((1, 1), jnp.float32),
        ],
        compiler_params=pltpu.CompilerParams(vmem_limit_bytes=VMEM),
        name="plan",
    )(counts)


def exchange(x, axis):
    return lax.all_to_all(x, axis, 0, 0, tiled=True)


def share(x, axis):
    return exchange(jnp.broadcast_to(x[None], (lax.axis_size(axis),) + x.shape), axis)


def seq_gather(x):
    swapped = lax.ppermute(x, "seq", [(i, i ^ 1) for i in range(N_SEQ)])
    x = jnp.stack([x, swapped])
    pieces = [x]
    for step in range(1, NEAR):
        pieces.append(far(x, step))
    return jnp.concatenate(pieces, axis=0)


def far(x, chips):
    return lax.ppermute(x, "seq", [(i, (i + 2 * chips) % N_SEQ) for i in range(N_SEQ)])


def body(queries, keys, values, d_out, cluster_id):
    seq = lax.axis_index("seq")
    tokens = queries.shape[0]
    member = (cluster_id == iota((1, CLUSTERS), 1)).astype(jnp.int32)
    own_counts, cluster_id = lax.optimization_barrier((jnp.sum(member, axis=0), cluster_id))
    member = (cluster_id == iota((1, CLUSTERS), 1)).astype(jnp.int32)
    running = jnp.cumsum(member, axis=0)
    ordinal = jnp.sum((running - 1) * member, axis=1)
    counts = share(own_counts[None].astype(jnp.float32), "seq")[:, 0]
    counts, ordinal = lax.optimization_barrier((counts, ordinal))
    planned, most = plan(counts)

    def with_rows(rows, queries, keys, values, d_out):
        sent, place = pack(
            seq.reshape(1, 1),
            planned,
            cluster_id.reshape(1, tokens),
            ordinal.reshape(1, tokens),
            (queries, keys, values, d_out),
            rows,
        )
        received = exchange(sent.reshape(N_SEQ, rows, 4 * DH), "seq")
        plan_whole = planned.astype(jnp.int32)
        start, owner, turn = plan_whole[:N_SEQ], plan_whole[N_SEQ], plan_whole[N_SEQ + 1]
        turns = jnp.arange(OWN, dtype=jnp.int32)
        mine = (owner[None, :] == seq) & (turn[None, :] == turns[:, None])
        here_counts = jnp.sum(jnp.where(mine[:, None, :], counts[None], 0.0), axis=2)
        here_start = jnp.sum(jnp.where(mine[:, None, :], start[None], 0), axis=2)
        slot = jnp.arange(CAPC, dtype=jnp.int32)
        taken = slot[None, None, :] < here_counts.astype(jnp.int32)[:, :, None]
        line = (jnp.arange(N_SEQ, dtype=jnp.int32) % GROUP) * rows
        spot = here_start[:, :, None] + slot[None, None, :] + line[None, :, None]
        spot = jnp.where(taken, spot, -1).reshape(OWN, GROUPS, PIECE)
        spot = spot.transpose(1, 0, 2).reshape(GROUPS, OWN * PIECE)
        spot, place = lax.optimization_barrier((spot, place.reshape(tokens, 1)))
        results = attention(spot, received.reshape(N_SEQ * rows, 4 * DH), rows)
        results, keys_in = lax.optimization_barrier((results, received[:, :, DH : 2 * DH]))
        returned = exchange(results.reshape(N_SEQ, rows, 4 * DH), "seq")
        key_rows = keys_in.astype(jnp.float32).reshape(N_SEQ * rows, DH)
        squares = jnp.sum(key_rows * key_rows, axis=1)
        norm = jnp.sum(lax.all_gather(squares, "head"), axis=0)
        row = jnp.arange(rows, dtype=jnp.int32)[None, None, :] - here_start[:, :, None]
        held = (row >= 0) & (row < here_counts.astype(jnp.int32)[:, :, None])
        held = held.reshape(OWN, N_SEQ * rows)
        unit = jnp.where(held, 1.0 / jnp.sqrt(norm / D + EPSILON)[None], 0.0)
        means = jnp.dot(unit, key_rows, precision=lax.Precision.HIGHEST)
        means = means / jnp.sum(here_counts, axis=1)[:, None]
        spread = jnp.sum(means * means, axis=1, keepdims=True)
        spread = lax.optimization_barrier(jnp.broadcast_to(spread, (OWN, DH)))
        spread = jnp.sum(lax.all_gather(spread, "head"), axis=0)
        near = seq_gather(means / jnp.sqrt(spread / D + EPSILON))
        back = lax.rem(N_SEQ // 2 + seq // 2 - owner // 2, N_SEQ // 2)
        entry = back * 2 + ((owner ^ seq) & 1)
        outs = unpack(place, returned.reshape(N_SEQ * rows, 4 * DH))
        near, outs = lax.optimization_barrier((near, outs))
        pieces = [near] + [far(near, step) for step in range(NEAR, N_SEQ // 2, NEAR)]
        every = jnp.concatenate(pieces, axis=0).reshape(-1, DH)
        centroids = every[entry * OWN + turn]
        return (*outs, centroids)

    return lax.cond(
        most[0, 0] <= ROWS_SHORT,
        functools.partial(with_rows, ROWS_SHORT),
        functools.partial(with_rows, ROWS_FULL),
        queries,
        keys,
        values,
        d_out,
    )


def solution(mesh):
    wide = P("seq", "head")
    return jax.shard_map(
        body,
        mesh=mesh,
        in_specs=(wide, wide, wide, wide, P("seq", None)),
        out_specs=(wide, wide, wide, wide, P(None, "head")),
        check_vma=False,
    )
```

```python
import functools

import jax
import jax.numpy as jnp
from jax import lax
from jax.experimental import pallas as pl
from jax.experimental.pallas import tpu as pltpu
from jax.sharding import PartitionSpec as P

DH = 128
CLUSTERS = 256
CAPC = 12
D = 2048
N_SEQ = 32
OWN = CLUSTERS // N_SEQ
SLOTS = N_SEQ * CAPC
GROUP = 4
GROUPS = N_SEQ // GROUP
PIECE = GROUP * CAPC
ROWS_SHORT = 72
ROWS_FULL = OWN * CAPC
PACK_STEPS = 4
EPSILON = 1e-06
NEAR = 6
HIDDEN = 1e30
LOG2E = 1.4426950408889634
SIDE_BY_SIDE = 4
TOGETHER = 4
VMEM = 24 * 1024 * 1024
VMEM_MOST = 60 * 1024 * 1024


def iota(shape, dim):
    return lax.broadcasted_iota(jnp.int32, shape, dim)


def one_hot(mask):
    return jnp.where(mask, 1.0, 0.0).astype(jnp.bfloat16)


def dot(a, b, ca, cb):
    return lax.dot_general(a, b, (((ca,), (cb,)), ((), ())), preferred_element_type=jnp.float32)


def pack_kernel(
    rows, seq_ref, plan_ref, cluster_ref, ordinal_ref, q_ref, k_ref, v_ref, g_ref,
    out_ref, place_ref, all_ref, part_ref, sem_ref,
):
    step = pl.program_id(0)
    part = N_SEQ // PACK_STEPS * rows

    @pl.when(step == 0)
    def _():
        for i, ref in enumerate((q_ref, k_ref, v_ref, g_ref)):
            all_ref[:, i * DH : (i + 1) * DH] = ref[...]
        chosen = (iota((N_SEQ, CLUSTERS), 0) == seq_ref[0, 0])
        start = jnp.sum(jnp.where(chosen, plan_ref[:N_SEQ], 0.0), axis=0, keepdims=True)
        owner = plan_ref[N_SEQ : N_SEQ + 1]
        table = jnp.where(iota((8, CLUSTERS), 0) == 0, owner, start).astype(jnp.bfloat16)
        tokens = cluster_ref.shape[1]
        member = one_hot(iota((CLUSTERS, tokens), 0) == cluster_ref[...])
        found = dot(table, member, 1, 0)
        place = found[0:1] * rows + found[1:2]
        place_ref[...] = place.astype(jnp.int32) + ordinal_ref[...]

    def copy(slot, at):
        return pltpu.make_async_copy(
            part_ref.at[slot], out_ref.at[pl.ds(pl.multiple_of(at * part, part), part)], sem_ref.at[slot]
        )

    slot = lax.rem(step, 2)

    @pl.when(step >= 2)
    def _():
        copy(slot, step - 2).wait()

    wanted = iota((part, place_ref.shape[1]), 0) + step * part
    part_ref[slot] = dot(one_hot(wanted == place_ref[...]), all_ref[...], 1, 0).astype(jnp.bfloat16)
    copy(slot, step).start()

    @pl.when(step == PACK_STEPS - 1)
    def _():
        copy(1 - slot, step - 1).wait()
        copy(slot, step).wait()


def pack(seq, planned, cluster_row, ordinal_row, arrays, rows):
    tokens = cluster_row.shape[1]

    def whole(*shape):
        return pl.BlockSpec(shape, lambda i: (0, 0))

    return pl.pallas_call(
        functools.partial(pack_kernel, rows),
        grid=(PACK_STEPS,),
        in_specs=[
            pl.BlockSpec(memory_space=pltpu.SMEM),
            whole(*planned.shape),
            whole(1, tokens),
            whole(1, tokens),
        ]
        + [whole(tokens, DH)] * 4,
        out_specs=[pl.BlockSpec(memory_space=pltpu.HBM), whole(1, tokens)],
        out_shape=[
            jax.ShapeDtypeStruct((N_SEQ * rows, 4 * DH), jnp.bfloat16),
            jax.ShapeDtypeStruct((1, tokens), jnp.int32),
        ],
        scratch_shapes=[
            pltpu.VMEM((tokens, 4 * DH), jnp.bfloat16),
            pltpu.VMEM((2, N_SEQ // PACK_STEPS * rows, 4 * DH), jnp.bfloat16),
            pltpu.SemaphoreType.DMA((2,)),
        ],
        compiler_params=pltpu.CompilerParams(vmem_limit_bytes=VMEM_MOST),
        name="pack",
    )(seq, planned, cluster_row, ordinal_row, *arrays)


def unpack_kernel(place_ref, in_ref, *out_refs):
    tokens = place_ref.shape[0]
    chosen = one_hot(place_ref[...] == iota((tokens, in_ref.shape[0]), 1))
    rows = dot(chosen, in_ref[...], 1, 0).astype(jnp.bfloat16)
    for i, ref in enumerate(out_refs):
        ref[...] = rows[:, i * DH : (i + 1) * DH]


def unpack(place_column, block):
    tokens = place_column.shape[0]
    tile = 512
    return pl.pallas_call(
        unpack_kernel,
        grid=(tokens // tile,),
        in_specs=[
            pl.BlockSpec((tile, 1), lambda i: (i, 0)),
            pl.BlockSpec(block.shape, lambda i: (0, 0)),
        ],
        out_specs=[pl.BlockSpec((tile, DH), lambda i: (i, 0))] * 4,
        out_shape=[jax.ShapeDtypeStruct((tokens, DH), jnp.bfloat16)] * 4,
        compiler_params=pltpu.CompilerParams(vmem_limit_bytes=VMEM),
        name="unpack",
    )(place_column, block)


def attention_kernel(rows, place_ref, in_ref, out_ref, x_ref, hide_ref, y_ref):
    part = GROUP * rows
    scaling = DH**-0.5

    def chosen(g):
        return one_hot(iota((part, OWN * PIECE), 0) == place_ref[pl.ds(g, 1), :])

    def several(work):
        def one(i, _):
            for j in range(SIDE_BY_SIDE):
                work(i * SIDE_BY_SIDE + j, 0)
            return 0

        return one

    def spread(g, _):
        block = in_ref[pl.ds(pl.multiple_of(g * part, part), part), :]
        block = jnp.concatenate([block, jnp.ones((part, DH), jnp.bfloat16)], axis=1)
        full = dot(chosen(g), block, 0, 0)
        moved = full[:, : 4 * DH].astype(jnp.bfloat16)
        hide = (full[:, 4 * DH :] - 1.0) * HIDDEN
        for k in range(OWN):
            at = pl.ds(pl.multiple_of(k * SLOTS + g * PIECE, 16), PIECE)
            x_ref[at, :] = moved[k * PIECE : (k + 1) * PIECE]
            hide_ref[at, :] = hide[k * PIECE : (k + 1) * PIECE]
        return 0

    lax.fori_loop(0, GROUPS // SIDE_BY_SIDE, several(spread), 0)
    causal = iota((DH, DH), 0) <= iota((DH, DH), 1)

    def attend(k):
        at = pl.ds(pl.multiple_of(k * SLOTS, SLOTS), SLOTS)
        query, key = x_ref[at, 0:DH], x_ref[at, DH : 2 * DH]
        value, grad = x_ref[at, 2 * DH : 3 * DH], x_ref[at, 3 * DH : 4 * DH]
        hide = hide_ref[at, :]
        weights_all, changes_all = [], []
        for i in range(SLOTS // DH):
            low, high = i * DH, (i + 1) * DH
            scores = dot(key[:high], query[low:high], 1, 1) * (scaling * LOG2E) + hide[:high]
            last = jnp.where(causal, scores[low:], -HIDDEN)
            scores = last if i == 0 else jnp.concatenate([scores[:low], last], axis=0)
            weights = jnp.exp2(scores - jnp.max(scores, axis=0, keepdims=True))
            attention = weights * (1.0 / jnp.sum(weights, axis=0, keepdims=True))
            grad_weights = dot(value[:high], grad[low:high], 1, 1)
            delta = jnp.sum(attention * grad_weights, axis=0, keepdims=True)
            weights_all.append(attention.astype(jnp.bfloat16))
            changes_all.append((attention * (grad_weights - delta)).astype(jnp.bfloat16))
        outs, grad_queries = [], []
        for i in range(SLOTS // DH):
            high = (i + 1) * DH
            outs.append(dot(weights_all[i], value[:high], 0, 0))
            grad_queries.append(dot(changes_all[i], key[:high], 0, 0) * scaling)
        grad_values, grad_keys = [], []
        for j in range(SLOTS // DH):
            row = slice(j * DH, (j + 1) * DH)
            rest = slice(j * DH, SLOTS)
            wide = jnp.concatenate([w[row] for w in weights_all[j:]], axis=1)
            grad_values.append(dot(wide, grad[rest], 1, 0))
            wide = jnp.concatenate([c[row] for c in changes_all[j:]], axis=1)
            grad_keys.append(dot(wide, query[rest], 1, 0) * scaling)
        for i, pieces in enumerate((outs, grad_queries, grad_keys, grad_values)):
            y_ref[at, i * DH : (i + 1) * DH] = jnp.concatenate(pieces, axis=0).astype(jnp.bfloat16)

    def attend_several(i, _):
        for j in range(TOGETHER):
            attend(i * TOGETHER + j)
        return 0

    lax.fori_loop(0, OWN // TOGETHER, attend_several, 0)

    def gather(g, _):
        pieces = [
            y_ref[pl.ds(pl.multiple_of(k * SLOTS + g * PIECE, 16), PIECE), :] for k in range(OWN)
        ]
        block = dot(chosen(g), jnp.concatenate(pieces, axis=0), 1, 0)
        out_ref[pl.ds(pl.multiple_of(g * part, part), part), :] = block.astype(jnp.bfloat16)
        return 0

    lax.fori_loop(0, GROUPS // SIDE_BY_SIDE, several(gather), 0)


def attention(places, block, rows):
    vmem = pl.BlockSpec(memory_space=pltpu.VMEM)
    return pl.pallas_call(
        functools.partial(attention_kernel, rows),
        in_specs=[vmem] * 2,
        out_specs=vmem,
        out_shape=jax.ShapeDtypeStruct(block.shape, jnp.bfloat16),
        scratch_shapes=[
            pltpu.VMEM((OWN * SLOTS, 4 * DH), jnp.bfloat16),
            pltpu.VMEM((OWN * SLOTS, DH), jnp.float32),
            pltpu.VMEM((OWN * SLOTS, 4 * DH), jnp.bfloat16),
        ],
        compiler_params=pltpu.CompilerParams(vmem_limit_bytes=VMEM),
        name="attention",
    )(places, block)


def across(x, step):
    low = (iota(x.shape, 1) & step) == 0
    return jnp.where(low, pltpu.roll(x, x.shape[1] - step, 1), pltpu.roll(x, step, 1))


def plan_kernel(counts_ref, out_ref, most_ref):
    counts = counts_ref[...]
    size_row = jnp.sum(counts, axis=0, keepdims=True)
    size_column = dot(counts.astype(jnp.bfloat16), jnp.ones((N_SEQ, CLUSTERS), jnp.bfloat16), 0, 0)
    square = (CLUSTERS, CLUSTERS)
    before = (size_column > size_row) | (
        (size_column == size_row) & (iota(square, 0) < iota(square, 1))
    )
    rank = jnp.sum(jnp.where(before, 1.0, 0.0), axis=0, keepdims=True).astype(jnp.int32)
    turn, spot = lax.shift_right_logical(rank, 5), rank & (N_SEQ - 1)
    owner = jnp.where((turn & 1) == 0, spot, N_SEQ - 1 - spot)
    number = iota((8, CLUSTERS), 1).astype(jnp.float32)
    named = jnp.concatenate([counts, number], axis=0).astype(jnp.bfloat16)
    tables = []
    for k in range(OWN):
        here = jnp.where(turn == k, owner, -1)
        tables.append(dot(named, one_hot(iota((DH, CLUSTERS), 0) == here), 1, 1))
    load = functools.reduce(jnp.add, [t[:N_SEQ] for t in tables])

    def cost(x):
        over = jnp.maximum(x - 60.0, 0.0)
        over = over * over
        return over * over

    for step in (1, 2, 4, 8, 16):
        other = across(load, step)
        for k in range(OWN):
            theirs = across(tables[k], step)
            change = theirs[:N_SEQ] - tables[k][:N_SEQ]
            more, less = load + change, other - change
            gain = (cost(more) + cost(less)) - (cost(load) + cost(other))
            swap = jnp.sum(gain, axis=0, keepdims=True) < 0.0
            load = jnp.where(swap, more, load)
            other = jnp.where(swap, less, other)
            tables[k] = jnp.where(swap, theirs, tables[k])
    owners = iota((N_SEQ, DH), 1)
    load = jnp.where(owners < N_SEQ, load, 0.0)
    most_ref[...] = jnp.max(jnp.max(load, axis=1, keepdims=True), axis=0, keepdims=True)
    start = jnp.zeros((N_SEQ, DH), jnp.float32)
    result = jnp.zeros((N_SEQ + 8, CLUSTERS), jnp.float32)
    for k in range(OWN):
        names = tables[k][N_SEQ : N_SEQ + 1]
        names = jnp.where(owners[:1] < N_SEQ, names, -1.0).astype(jnp.int32)
        extra = jnp.where(iota((8, DH), 0) == 0, iota((8, DH), 1), k).astype(jnp.float32)
        values = jnp.concatenate([start, extra], axis=0).astype(jnp.bfloat16)
        result += dot(values, one_hot(iota((CLUSTERS, DH), 0) == names), 1, 1)
        start = start + tables[k][:N_SEQ]
    out_ref[...] = result


def plan(counts):
    return pl.pallas_call(
        plan_kernel,
        out_shape=[
            jax.ShapeDtypeStruct((N_SEQ + 8, CLUSTERS), jnp.float32),
            jax.ShapeDtypeStruct((1, 1), jnp.float32),
        ],
        compiler_params=pltpu.CompilerParams(vmem_limit_bytes=VMEM),
        name="plan",
    )(counts)


def exchange(x, axis):
    return lax.all_to_all(x, axis, 0, 0, tiled=True)


def share(x, axis):
    return exchange(jnp.broadcast_to(x[None], (lax.axis_size(axis),) + x.shape), axis)


def seq_gather(x):
    swapped = lax.ppermute(x, "seq", [(i, i ^ 1) for i in range(N_SEQ)])
    x = jnp.stack([x, swapped])
    pieces = [x]
    for step in range(1, NEAR):
        pieces.append(far(x, step))
    return jnp.concatenate(pieces, axis=0)


def far(x, chips):
    return lax.ppermute(x, "seq", [(i, (i + 2 * chips) % N_SEQ) for i in range(N_SEQ)])


def body(queries, keys, values, d_out, cluster_id):
    seq = lax.axis_index("seq")
    tokens = queries.shape[0]
    member = (cluster_id == iota((1, CLUSTERS), 1)).astype(jnp.int32)
    own_counts, cluster_id = lax.optimization_barrier((jnp.sum(member, axis=0), cluster_id))
    member = (cluster_id == iota((1, CLUSTERS), 1)).astype(jnp.int32)
    running = jnp.cumsum(member, axis=0)
    ordinal = jnp.sum((running - 1) * member, axis=1)
    counts = share(own_counts[None].astype(jnp.float32), "seq")[:, 0]
    counts, ordinal = lax.optimization_barrier((counts, ordinal))
    planned, most = plan(counts)

    def with_rows(rows, queries, keys, values, d_out):
        sent, place = pack(
            seq.reshape(1, 1),
            planned,
            cluster_id.reshape(1, tokens),
            ordinal.reshape(1, tokens),
            (queries, keys, values, d_out),
            rows,
        )
        received = exchange(sent.reshape(N_SEQ, rows, 4 * DH), "seq")
        plan_whole = planned.astype(jnp.int32)
        start, owner, turn = plan_whole[:N_SEQ], plan_whole[N_SEQ], plan_whole[N_SEQ + 1]
        turns = jnp.arange(OWN, dtype=jnp.int32)
        mine = (owner[None, :] == seq) & (turn[None, :] == turns[:, None])
        here_counts = jnp.sum(jnp.where(mine[:, None, :], counts[None], 0.0), axis=2)
        here_start = jnp.sum(jnp.where(mine[:, None, :], start[None], 0), axis=2)
        slot = jnp.arange(CAPC, dtype=jnp.int32)
        taken = slot[None, None, :] < here_counts.astype(jnp.int32)[:, :, None]
        line = (jnp.arange(N_SEQ, dtype=jnp.int32) % GROUP) * rows
        spot = here_start[:, :, None] + slot[None, None, :] + line[None, :, None]
        spot = jnp.where(taken, spot, -1).reshape(OWN, GROUPS, PIECE)
        spot = spot.transpose(1, 0, 2).reshape(GROUPS, OWN * PIECE)
        spot, place = lax.optimization_barrier((spot, place.reshape(tokens, 1)))
        results = attention(spot, received.reshape(N_SEQ * rows, 4 * DH), rows)
        results, keys_in = lax.optimization_barrier((results, received[:, :, DH : 2 * DH]))
        returned = exchange(results.reshape(N_SEQ, rows, 4 * DH), "seq")
        key_rows = keys_in.astype(jnp.float32).reshape(N_SEQ * rows, DH)
        squares = jnp.sum(key_rows * key_rows, axis=1)
        norm = jnp.sum(lax.all_gather(squares, "head"), axis=0)
        row = jnp.arange(rows, dtype=jnp.int32)[None, None, :] - here_start[:, :, None]
        held = (row >= 0) & (row < here_counts.astype(jnp.int32)[:, :, None])
        held = held.reshape(OWN, N_SEQ * rows)
        unit = jnp.where(held, 1.0 / jnp.sqrt(norm / D + EPSILON)[None], 0.0)
        means = jnp.dot(unit, key_rows, precision=lax.Precision.HIGHEST)
        means = means / jnp.sum(here_counts, axis=1)[:, None]
        spread = jnp.sum(means * means, axis=1, keepdims=True)
        spread = lax.optimization_barrier(jnp.broadcast_to(spread, (OWN, DH)))
        spread = jnp.sum(lax.all_gather(spread, "head"), axis=0)
        near = seq_gather(means / jnp.sqrt(spread / D + EPSILON))
        back = lax.rem(N_SEQ // 2 + seq // 2 - owner // 2, N_SEQ // 2)
        entry = back * 2 + ((owner ^ seq) & 1)
        outs = unpack(place, returned.reshape(N_SEQ * rows, 4 * DH))
        near, outs = lax.optimization_barrier((near, outs))
        pieces = [near] + [far(near, step) for step in range(NEAR, N_SEQ // 2, NEAR)]
        every = jnp.concatenate(pieces, axis=0).reshape(-1, DH)
        centroids = every[entry * OWN + turn]
        return (*outs, centroids)

    return lax.cond(
        most[0, 0] <= ROWS_SHORT,
        functools.partial(with_rows, ROWS_SHORT),
        functools.partial(with_rows, ROWS_FULL),
        queries,
        keys,
        values,
        d_out,
    )


def solution(mesh):
    wide = P("seq", "head")
    return jax.shard_map(
        body,
        mesh=mesh,
        in_specs=(wide, wide, wide, wide, P("seq", None)),
        out_specs=(wide, wide, wide, wide, P(None, "head")),
        check_vma=False,
    )
```

```python
import functools

import jax
import jax.numpy as jnp
from jax import lax
from jax.experimental import pallas as pl
from jax.experimental.pallas import tpu as pltpu
from jax.sharding import PartitionSpec as P

DH = 128
CLUSTERS = 256
CAPC = 12
D = 2048
N_SEQ = 32
OWN = CLUSTERS // N_SEQ
SLOTS = N_SEQ * CAPC
GROUP = 4
GROUPS = N_SEQ // GROUP
PIECE = GROUP * CAPC
ROWS_SHORT = 72
ROWS_FULL = OWN * CAPC
PACK_STEPS = 4
EPSILON = 1e-06
NEAR = 8
HIDDEN = 1e30
LOG2E = 1.4426950408889634
SIDE_BY_SIDE = 4
TOGETHER = 4
VMEM = 24 * 1024 * 1024
VMEM_MOST = 60 * 1024 * 1024


def iota(shape, dim):
    return lax.broadcasted_iota(jnp.int32, shape, dim)


def one_hot(mask):
    return jnp.where(mask, 1.0, 0.0).astype(jnp.bfloat16)


def dot(a, b, ca, cb):
    return lax.dot_general(a, b, (((ca,), (cb,)), ((), ())), preferred_element_type=jnp.float32)


def pack_kernel(
    rows, seq_ref, plan_ref, cluster_ref, ordinal_ref, q_ref, k_ref, v_ref, g_ref,
    out_ref, place_ref, all_ref, part_ref, sem_ref,
):
    step = pl.program_id(0)
    part = N_SEQ // PACK_STEPS * rows

    @pl.when(step == 0)
    def _():
        for i, ref in enumerate((q_ref, k_ref, v_ref, g_ref)):
            all_ref[:, i * DH : (i + 1) * DH] = ref[...]
        chosen = (iota((N_SEQ, CLUSTERS), 0) == seq_ref[0, 0])
        start = jnp.sum(jnp.where(chosen, plan_ref[:N_SEQ], 0.0), axis=0, keepdims=True)
        owner = plan_ref[N_SEQ : N_SEQ + 1]
        table = jnp.where(iota((8, CLUSTERS), 0) == 0, owner, start).astype(jnp.bfloat16)
        tokens = cluster_ref.shape[1]
        member = one_hot(iota((CLUSTERS, tokens), 0) == cluster_ref[...])
        found = dot(table, member, 1, 0)
        place = found[0:1] * rows + found[1:2]
        place_ref[...] = place.astype(jnp.int32) + ordinal_ref[...]

    def copy(slot, at):
        return pltpu.make_async_copy(
            part_ref.at[slot], out_ref.at[pl.ds(pl.multiple_of(at * part, part), part)], sem_ref.at[slot]
        )

    slot = lax.rem(step, 2)

    @pl.when(step >= 2)
    def _():
        copy(slot, step - 2).wait()

    wanted = iota((part, place_ref.shape[1]), 0) + step * part
    part_ref[slot] = dot(one_hot(wanted == place_ref[...]), all_ref[...], 1, 0).astype(jnp.bfloat16)
    copy(slot, step).start()

    @pl.when(step == PACK_STEPS - 1)
    def _():
        copy(1 - slot, step - 1).wait()
        copy(slot, step).wait()


def pack(seq, planned, cluster_row, ordinal_row, arrays, rows):
    tokens = cluster_row.shape[1]

    def whole(*shape):
        return pl.BlockSpec(shape, lambda i: (0, 0))

    return pl.pallas_call(
        functools.partial(pack_kernel, rows),
        grid=(PACK_STEPS,),
        in_specs=[
            pl.BlockSpec(memory_space=pltpu.SMEM),
            whole(*planned.shape),
            whole(1, tokens),
            whole(1, tokens),
        ]
        + [whole(tokens, DH)] * 4,
        out_specs=[pl.BlockSpec(memory_space=pltpu.HBM), whole(1, tokens)],
        out_shape=[
            jax.ShapeDtypeStruct((N_SEQ * rows, 4 * DH), jnp.bfloat16),
            jax.ShapeDtypeStruct((1, tokens), jnp.int32),
        ],
        scratch_shapes=[
            pltpu.VMEM((tokens, 4 * DH), jnp.bfloat16),
            pltpu.VMEM((2, N_SEQ // PACK_STEPS * rows, 4 * DH), jnp.bfloat16),
            pltpu.SemaphoreType.DMA((2,)),
        ],
        compiler_params=pltpu.CompilerParams(vmem_limit_bytes=VMEM_MOST),
        name="pack",
    )(seq, planned, cluster_row, ordinal_row, *arrays)


def unpack_kernel(place_ref, in_ref, *out_refs):
    tokens = place_ref.shape[0]
    chosen = one_hot(place_ref[...] == iota((tokens, in_ref.shape[0]), 1))
    rows = dot(chosen, in_ref[...], 1, 0).astype(jnp.bfloat16)
    for i, ref in enumerate(out_refs):
        ref[...] = rows[:, i * DH : (i + 1) * DH]


def unpack(place_column, block):
    tokens = place_column.shape[0]
    tile = 512
    return pl.pallas_call(
        unpack_kernel,
        grid=(tokens // tile,),
        in_specs=[
            pl.BlockSpec((tile, 1), lambda i: (i, 0)),
            pl.BlockSpec(block.shape, lambda i: (0, 0)),
        ],
        out_specs=[pl.BlockSpec((tile, DH), lambda i: (i, 0))] * 4,
        out_shape=[jax.ShapeDtypeStruct((tokens, DH), jnp.bfloat16)] * 4,
        compiler_params=pltpu.CompilerParams(vmem_limit_bytes=VMEM),
        name="unpack",
    )(place_column, block)


def attention_kernel(rows, place_ref, in_ref, out_ref, x_ref, hide_ref, y_ref):
    part = GROUP * rows
    scaling = DH**-0.5

    def chosen(g):
        return one_hot(iota((part, OWN * PIECE), 0) == place_ref[pl.ds(g, 1), :])

    def several(work):
        def one(i, _):
            for j in range(SIDE_BY_SIDE):
                work(i * SIDE_BY_SIDE + j, 0)
            return 0

        return one

    def spread(g, _):
        block = in_ref[pl.ds(pl.multiple_of(g * part, part), part), :]
        block = jnp.concatenate([block, jnp.ones((part, DH), jnp.bfloat16)], axis=1)
        full = dot(chosen(g), block, 0, 0)
        moved = full[:, : 4 * DH].astype(jnp.bfloat16)
        hide = (full[:, 4 * DH :] - 1.0) * HIDDEN
        for k in range(OWN):
            at = pl.ds(pl.multiple_of(k * SLOTS + g * PIECE, 16), PIECE)
            x_ref[at, :] = moved[k * PIECE : (k + 1) * PIECE]
            hide_ref[at, :] = hide[k * PIECE : (k + 1) * PIECE]
        return 0

    lax.fori_loop(0, GROUPS // SIDE_BY_SIDE, several(spread), 0)
    causal = iota((DH, DH), 0) <= iota((DH, DH), 1)

    def attend(k):
        at = pl.ds(pl.multiple_of(k * SLOTS, SLOTS), SLOTS)
        query, key = x_ref[at, 0:DH], x_ref[at, DH : 2 * DH]
        value, grad = x_ref[at, 2 * DH : 3 * DH], x_ref[at, 3 * DH : 4 * DH]
        hide = hide_ref[at, :]
        weights_all, changes_all = [], []
        for i in range(SLOTS // DH):
            low, high = i * DH, (i + 1) * DH
            scores = dot(key[:high], query[low:high], 1, 1) * (scaling * LOG2E) + hide[:high]
            last = jnp.where(causal, scores[low:], -HIDDEN)
            scores = last if i == 0 else jnp.concatenate([scores[:low], last], axis=0)
            weights = jnp.exp2(scores - jnp.max(scores, axis=0, keepdims=True))
            attention = weights * (1.0 / jnp.sum(weights, axis=0, keepdims=True))
            grad_weights = dot(value[:high], grad[low:high], 1, 1)
            delta = jnp.sum(attention * grad_weights, axis=0, keepdims=True)
            weights_all.append(attention.astype(jnp.bfloat16))
            changes_all.append((attention * (grad_weights - delta)).astype(jnp.bfloat16))
        outs, grad_queries = [], []
        for i in range(SLOTS // DH):
            high = (i + 1) * DH
            outs.append(dot(weights_all[i], value[:high], 0, 0))
            grad_queries.append(dot(changes_all[i], key[:high], 0, 0) * scaling)
        grad_values, grad_keys = [], []
        for j in range(SLOTS // DH):
            row = slice(j * DH, (j + 1) * DH)
            rest = slice(j * DH, SLOTS)
            wide = jnp.concatenate([w[row] for w in weights_all[j:]], axis=1)
            grad_values.append(dot(wide, grad[rest], 1, 0))
            wide = jnp.concatenate([c[row] for c in changes_all[j:]], axis=1)
            grad_keys.append(dot(wide, query[rest], 1, 0) * scaling)
        for i, pieces in enumerate((outs, grad_queries, grad_keys, grad_values)):
            y_ref[at, i * DH : (i + 1) * DH] = jnp.concatenate(pieces, axis=0).astype(jnp.bfloat16)

    def attend_several(i, _):
        for j in range(TOGETHER):
            attend(i * TOGETHER + j)
        return 0

    lax.fori_loop(0, OWN // TOGETHER, attend_several, 0)

    def gather(g, _):
        pieces = [
            y_ref[pl.ds(pl.multiple_of(k * SLOTS + g * PIECE, 16), PIECE), :] for k in range(OWN)
        ]
        block = dot(chosen(g), jnp.concatenate(pieces, axis=0), 1, 0)
        out_ref[pl.ds(pl.multiple_of(g * part, part), part), :] = block.astype(jnp.bfloat16)
        return 0

    lax.fori_loop(0, GROUPS // SIDE_BY_SIDE, several(gather), 0)


def attention(places, block, rows):
    vmem = pl.BlockSpec(memory_space=pltpu.VMEM)
    return pl.pallas_call(
        functools.partial(attention_kernel, rows),
        in_specs=[vmem] * 2,
        out_specs=vmem,
        out_shape=jax.ShapeDtypeStruct(block.shape, jnp.bfloat16),
        scratch_shapes=[
            pltpu.VMEM((OWN * SLOTS, 4 * DH), jnp.bfloat16),
            pltpu.VMEM((OWN * SLOTS, DH), jnp.float32),
            pltpu.VMEM((OWN * SLOTS, 4 * DH), jnp.bfloat16),
        ],
        compiler_params=pltpu.CompilerParams(vmem_limit_bytes=VMEM),
        name="attention",
    )(places, block)


def across(x, step):
    low = (iota(x.shape, 1) & step) == 0
    return jnp.where(low, pltpu.roll(x, x.shape[1] - step, 1), pltpu.roll(x, step, 1))


def plan_kernel(counts_ref, out_ref, most_ref):
    counts = counts_ref[...]
    size_row = jnp.sum(counts, axis=0, keepdims=True)
    size_column = dot(counts.astype(jnp.bfloat16), jnp.ones((N_SEQ, CLUSTERS), jnp.bfloat16), 0, 0)
    square = (CLUSTERS, CLUSTERS)
    before = (size_column > size_row) | (
        (size_column == size_row) & (iota(square, 0) < iota(square, 1))
    )
    rank = jnp.sum(jnp.where(before, 1.0, 0.0), axis=0, keepdims=True).astype(jnp.int32)
    turn, spot = lax.shift_right_logical(rank, 5), rank & (N_SEQ - 1)
    owner = jnp.where((turn & 1) == 0, spot, N_SEQ - 1 - spot)
    number = iota((8, CLUSTERS), 1).astype(jnp.float32)
    named = jnp.concatenate([counts, number], axis=0).astype(jnp.bfloat16)
    tables = []
    for k in range(OWN):
        here = jnp.where(turn == k, owner, -1)
        tables.append(dot(named, one_hot(iota((DH, CLUSTERS), 0) == here), 1, 1))
    load = functools.reduce(jnp.add, [t[:N_SEQ] for t in tables])

    def cost(x):
        over = jnp.maximum(x - 60.0, 0.0)
        over = over * over
        return over * over

    for step in (1, 2, 4, 8, 16):
        other = across(load, step)
        for k in range(OWN):
            theirs = across(tables[k], step)
            change = theirs[:N_SEQ] - tables[k][:N_SEQ]
            more, less = load + change, other - change
            gain = (cost(more) + cost(less)) - (cost(load) + cost(other))
            swap = jnp.sum(gain, axis=0, keepdims=True) < 0.0
            load = jnp.where(swap, more, load)
            other = jnp.where(swap, less, other)
            tables[k] = jnp.where(swap, theirs, tables[k])
    owners = iota((N_SEQ, DH), 1)
    load = jnp.where(owners < N_SEQ, load, 0.0)
    most_ref[...] = jnp.max(jnp.max(load, axis=1, keepdims=True), axis=0, keepdims=True)
    start = jnp.zeros((N_SEQ, DH), jnp.float32)
    result = jnp.zeros((N_SEQ + 8, CLUSTERS), jnp.float32)
    for k in range(OWN):
        names = tables[k][N_SEQ : N_SEQ + 1]
        names = jnp.where(owners[:1] < N_SEQ, names, -1.0).astype(jnp.int32)
        extra = jnp.where(iota((8, DH), 0) == 0, iota((8, DH), 1), k).astype(jnp.float32)
        values = jnp.concatenate([start, extra], axis=0).astype(jnp.bfloat16)
        result += dot(values, one_hot(iota((CLUSTERS, DH), 0) == names), 1, 1)
        start = start + tables[k][:N_SEQ]
    out_ref[...] = result


def plan(counts):
    return pl.pallas_call(
        plan_kernel,
        out_shape=[
            jax.ShapeDtypeStruct((N_SEQ + 8, CLUSTERS), jnp.float32),
            jax.ShapeDtypeStruct((1, 1), jnp.float32),
        ],
        compiler_params=pltpu.CompilerParams(vmem_limit_bytes=VMEM),
        name="plan",
    )(counts)


def exchange(x, axis):
    return lax.all_to_all(x, axis, 0, 0, tiled=True)


def share(x, axis):
    return exchange(jnp.broadcast_to(x[None], (lax.axis_size(axis),) + x.shape), axis)


def seq_gather(x):
    swapped = lax.ppermute(x, "seq", [(i, i ^ 1) for i in range(N_SEQ)])
    x = jnp.stack([x, swapped])
    pieces = [x]
    for step in range(1, NEAR):
        pieces.append(far(x, step))
    return jnp.concatenate(pieces, axis=0)


def far(x, chips):
    return lax.ppermute(x, "seq", [(i, (i + 2 * chips) % N_SEQ) for i in range(N_SEQ)])


def body(queries, keys, values, d_out, cluster_id):
    seq = lax.axis_index("seq")
    tokens = queries.shape[0]
    member = (cluster_id == iota((1, CLUSTERS), 1)).astype(jnp.int32)
    own_counts, cluster_id = lax.optimization_barrier((jnp.sum(member, axis=0), cluster_id))
    member = (cluster_id == iota((1, CLUSTERS), 1)).astype(jnp.int32)
    running = jnp.cumsum(member, axis=0)
    ordinal = jnp.sum((running - 1) * member, axis=1)
    counts = share(own_counts[None].astype(jnp.float32), "seq")[:, 0]
    counts, ordinal = lax.optimization_barrier((counts, ordinal))
    planned, most = plan(counts)

    def with_rows(rows, queries, keys, values, d_out):
        sent, place = pack(
            seq.reshape(1, 1),
            planned,
            cluster_id.reshape(1, tokens),
            ordinal.reshape(1, tokens),
            (queries, keys, values, d_out),
            rows,
        )
        received = exchange(sent.reshape(N_SEQ, rows, 4 * DH), "seq")
        plan_whole = planned.astype(jnp.int32)
        start, owner, turn = plan_whole[:N_SEQ], plan_whole[N_SEQ], plan_whole[N_SEQ + 1]
        turns = jnp.arange(OWN, dtype=jnp.int32)
        mine = (owner[None, :] == seq) & (turn[None, :] == turns[:, None])
        here_counts = jnp.sum(jnp.where(mine[:, None, :], counts[None], 0.0), axis=2)
        here_start = jnp.sum(jnp.where(mine[:, None, :], start[None], 0), axis=2)
        slot = jnp.arange(CAPC, dtype=jnp.int32)
        taken = slot[None, None, :] < here_counts.astype(jnp.int32)[:, :, None]
        line = (jnp.arange(N_SEQ, dtype=jnp.int32) % GROUP) * rows
        spot = here_start[:, :, None] + slot[None, None, :] + line[None, :, None]
        spot = jnp.where(taken, spot, -1).reshape(OWN, GROUPS, PIECE)
        spot = spot.transpose(1, 0, 2).reshape(GROUPS, OWN * PIECE)
        spot, place = lax.optimization_barrier((spot, place.reshape(tokens, 1)))
        results = attention(spot, received.reshape(N_SEQ * rows, 4 * DH), rows)
        results, keys_in = lax.optimization_barrier((results, received[:, :, DH : 2 * DH]))
        returned = exchange(results.reshape(N_SEQ, rows, 4 * DH), "seq")
        key_rows = keys_in.astype(jnp.float32).reshape(N_SEQ * rows, DH)
        squares = jnp.sum(key_rows * key_rows, axis=1)
        norm = jnp.sum(lax.all_gather(squares, "head"), axis=0)
        row = jnp.arange(rows, dtype=jnp.int32)[None, None, :] - here_start[:, :, None]
        held = (row >= 0) & (row < here_counts.astype(jnp.int32)[:, :, None])
        held = held.reshape(OWN, N_SEQ * rows)
        unit = jnp.where(held, 1.0 / jnp.sqrt(norm / D + EPSILON)[None], 0.0)
        means = jnp.dot(unit, key_rows, precision=lax.Precision.HIGHEST)
        means = means / jnp.sum(here_counts, axis=1)[:, None]
        spread = jnp.sum(means * means, axis=1, keepdims=True)
        spread = lax.optimization_barrier(jnp.broadcast_to(spread, (OWN, DH)))
        spread = jnp.sum(lax.all_gather(spread, "head"), axis=0)
        near = seq_gather(means / jnp.sqrt(spread / D + EPSILON))
        back = lax.rem(N_SEQ // 2 + seq // 2 - owner // 2, N_SEQ // 2)
        entry = back * 2 + ((owner ^ seq) & 1)
        outs = unpack(place, returned.reshape(N_SEQ * rows, 4 * DH))
        near, outs = lax.optimization_barrier((near, outs))
        pieces = [near] + [far(near, step) for step in range(NEAR, N_SEQ // 2, NEAR)]
        every = jnp.concatenate(pieces, axis=0).reshape(-1, DH)
        centroids = every[entry * OWN + turn]
        return (*outs, centroids)

    return lax.cond(
        most[0, 0] <= ROWS_SHORT,
        functools.partial(with_rows, ROWS_SHORT),
        functools.partial(with_rows, ROWS_FULL),
        queries,
        keys,
        values,
        d_out,
    )


def solution(mesh):
    wide = P("seq", "head")
    return jax.shard_map(
        body,
        mesh=mesh,
        in_specs=(wide, wide, wide, wide, P("seq", None)),
        out_specs=(wide, wide, wide, wide, P(None, "head")),
        check_vma=False,
    )
```
